128 devices in a mesh: row: 8 (over z, core), col: 16 (over x, y).
Axes of the slice: x: 4, y: 4, z: 4, core: 2. Of those that a mesh axis runs over, the one named last changes fastest.
Arguments:
- tensor: bfloat16 [128, 1024, 4096], P('row', 'col'), may hold values from -6 to 6
- pair_mu: int32 [1024], P('col'), may hold values from 0 to 15, as said below
- pair_nu: int32 [1024], P('col'), may hold values from 0 to 127, as said below
- occ_density: bfloat16 [8192, 384], replicated, may hold values from -0.09375 to 0.09375
- virt_density: bfloat16 [1024, 128], P('row'), may hold values from -0.5 to 0.5
Outputs:
- transformed: bfloat16 [8, 16, 1024, 384], P(None, 'col', 'row')
The draws below stay inside these ranges and needn't reach their ends.
Inputs may be any that keep to these rules, and one draw needn't show every extreme that they name: `pair_mu`: within the 64 pairs of one index of col (aligned runs of the list), at most 8 pairs name one mu block, and in every such run some mu block is named by exactly 8. `pair_nu`: no two pairs name the same mu block and the same nu block.
All inputs are finite; a program needn't handle non-finite values.
Results may differ from the reference program's by a relative error of at most 0.005.
Values may be sent and summed in bfloat16 or wider, within the bound.
A program may use at most 192 MiB of HBM per device.

```python
import jax
import jax.numpy as jnp
from jax import lax

BS = 64
CAPM = 8
PAIR_C = 64
NBNU = 128
NNU = 384
AUX_R = 16
NMB = 16
AUX = 128
NPAIR = 1024
N_ROW = 8
N_COL = 16


def pattern(key):
    key_hot, key_cols, key_perm = jax.random.split(key, 3)
    hot_blocks = jax.random.randint(key_hot, (N_COL,), 0, NMB)

    def one_column(column_key, hot_block):
        key_order, key_place = jax.random.split(column_key)
        order = jax.random.permutation(key_order, (NMB - 1) * CAPM)[:PAIR_C - CAPM]
        others = order // CAPM
        others = others + (others >= hot_block).astype(jnp.int32)
        blocks = jnp.concatenate([jnp.full((CAPM,), hot_block, jnp.int32), others.astype(jnp.int32)])
        shuffle = jax.random.permutation(key_place, PAIR_C)
        return blocks[shuffle]
    column_keys = jax.random.split(key_cols, N_COL)
    mu_ids = jax.vmap(one_column)(column_keys, hot_blocks).reshape(-1).astype(jnp.int32)
    member = (mu_ids[:, None] == jnp.arange(NMB, dtype=jnp.int32)[None, :]).astype(jnp.int32)
    ranking = jnp.sum(member * (jnp.cumsum(member, axis=0) - 1), axis=1)
    perm_keys = jax.random.split(key_perm, NMB)
    perms = jax.vmap(lambda k: jax.random.permutation(k, NBNU))(perm_keys).astype(jnp.int32)
    nu_ids = perms[mu_ids, ranking].astype(jnp.int32)
    return (mu_ids, nu_ids)


def draw_pair_mu(key, part):
    mu_ids, nu_ids = pattern(key)
    return mu_ids


def draw_pair_nu(key, part):
    mu_ids, nu_ids = pattern(key)
    return nu_ids


def block_levels(own_key, shape, cuts, least, largest):
    def one(position, parts):
        draws = jax.random.uniform(jax.random.fold_in(jax.random.fold_in(own_key, 6), position), (parts,), jnp.float32, least / len(cuts), largest / len(cuts))
        return jnp.repeat(jnp.exp(draws), shape[position] // parts).reshape((-1,) + (1,) * (len(shape) - position - 1))

    level = one(*cuts[0])
    for cut in cuts[1:]:
        level = level * one(*cut)
    return level


def scatter_about(stream_key, dims, width, most, cuts=(), kind=jnp.bfloat16):
    array = jax.random.normal(stream_key, dims, jnp.float32) * width
    if len(cuts) > 0:
        array = block_levels(stream_key, dims, cuts, -0.22, 0.18) * array
    return jnp.clip(array, min=-most, max=most).astype(kind)


def setup_inputs(seed: int = 0) -> dict:
    streams_of = jax.random.split(jax.random.key(seed), 6)
    return {
        "tensor": scatter_about(streams_of[0], (AUX, NPAIR, BS * BS), 1.0, 6.0, ((0, 8), (1, 16))),
        "pair_mu": draw_pair_mu(jax.random.fold_in(streams_of[5], 71), 0),
        "pair_nu": draw_pair_nu(jax.random.fold_in(streams_of[5], 71), 0),
        "occ_density": scatter_about(streams_of[3], (NBNU * BS, NNU), (N_COL * CAPM * BS // 2) ** -0.5, 0.09375),
        "virt_density": scatter_about(streams_of[4], (NMB * BS, 2 * BS), (2 * BS) ** -0.5, 0.5, ((0, 8),)),
    }


def reference(tensor, pair_mu, pair_nu, occ_density, virt_density):
    occ_table = occ_density.reshape(NBNU, BS, NNU)
    aux_total = tensor.shape[0]
    zero_index = jnp.zeros((), jnp.int32)

    def add_pair(index, carry):
        where = jnp.asarray(index).astype(jnp.int32)
        piece = lax.dynamic_index_in_dim(tensor, where, 1, keepdims=False).reshape(aux_total * BS, BS)
        density_rows = lax.dynamic_index_in_dim(occ_table, pair_nu[where], 0, keepdims=False)
        product = jnp.dot(piece, density_rows, preferred_element_type=jnp.float32).reshape(aux_total, 1, BS, NNU)
        block_index = pair_mu[where].astype(jnp.int32)
        starts = (zero_index, block_index, zero_index, zero_index)
        current = lax.dynamic_slice(carry, starts, (aux_total, 1, BS, NNU))
        return lax.dynamic_update_slice(carry, current + product, starts)

    half = jnp.zeros((aux_total, NMB, BS, NNU), jnp.float32)
    half = lax.fori_loop(0, NPAIR, add_pair, half)
    half_bf = lax.optimization_barrier(half.astype(jnp.bfloat16))
    grouped = half_bf.astype(jnp.float32).reshape(aux_total, N_ROW, 2 * BS, NNU)
    virt_blocks = virt_density.astype(jnp.float32).reshape(N_ROW, 2 * BS, 2 * BS)
    full = jnp.einsum("rki,prin->prkn", virt_blocks, grouped)
    return full.reshape(N_ROW, AUX_R, NMB * BS, NNU).astype(jnp.bfloat16)
```

```python
import jax
import jax.numpy as jnp
from jax import lax
from jax.experimental import pallas as pl
from jax.experimental.pallas import tpu as pltpu
from jax.sharding import PartitionSpec as P

MESH = pl.DeviceIdType.MESH
BS = 64
NNU = 384
NBNU = 128
NMB = 16
CAPM = 8
PAIRS = 64
HALF = 2048
ORDER = (2, 1, 3, 0)
F32 = jnp.float32
BF16 = jnp.bfloat16


def slot_table(mu_row, nu_row):
    sub = lax.broadcasted_iota(jnp.int32, (PAIRS, PAIRS), 0)
    lane = lax.broadcasted_iota(jnp.int32, (PAIRS, PAIRS), 1)
    mu_b = jnp.broadcast_to(mu_row, (PAIRS, PAIRS))
    nu_b = jnp.broadcast_to(nu_row, (PAIRS, PAIRS))
    mu_col = jnp.sum(jnp.where(sub == lane, mu_b, 0), axis=1, keepdims=True)
    nu_col = jnp.sum(jnp.where(sub == lane, nu_b, 0), axis=1, keepdims=True)
    rank = jnp.sum(jnp.where((mu_b == mu_col) & (lane < sub), 1, 0), axis=1, keepdims=True)
    slot = lax.broadcasted_iota(jnp.int32, (PAIRS, NMB * CAPM), 1)
    pair = lax.broadcasted_iota(jnp.int32, (PAIRS, NMB * CAPM), 0)
    hit = (mu_col * CAPM + rank) == slot
    source = jnp.sum(jnp.where(hit, pair, 0), axis=0, keepdims=True)
    target = jnp.sum(jnp.where(hit, nu_col - NBNU, 0), axis=0, keepdims=True) + NBNU
    row = lax.broadcasted_iota(jnp.int32, (8, NMB * CAPM), 0)
    return jnp.where(row == 0, source, target)


def kernel(t_ref, mu_ref, nu_ref, occ_ref, virt_ref, o_ref,
           arrived, occ, zbuf, xt, sums, sbuf, rbuf, hbuf, gbuf, tab_v, tab_r, tab_s,
           occ_sem, own_sem, s1, r1, st, rt, tab_sem, s2, r2, s3, r3, loc_sem):
    row, col = lax.axis_index("row"), lax.axis_index("col")
    x, y, z, core = col // 4, col % 4, row // 2, row % 2

    def at_x(d):
        return (row, lax.rem(x + d, 4) * 4 + y)

    def at_y(d):
        return (row, x * 4 + lax.rem(y + d, 4))

    def ring(h, d):
        return at_x(d) if h == 0 else at_y(d)

    occ_copy = pltpu.make_async_copy(occ_ref, occ.at[pl.ds(0, NBNU)], occ_sem)
    occ_copy.start()

    def piece(h, d):
        if h == 0:
            return t_ref.at[lax.rem(x + d, 4), :, :, pl.ds(0, HALF)]
        return t_ref.at[:, lax.rem(y + d, 4), :, pl.ds(HALF, HALF)]

    own = []
    for h in range(2):
        copy = pltpu.make_async_copy(piece(h, 0), arrived.at[h], own_sem.at[h])
        copy.start()
        own.append(copy)

    barrier = pltpu.get_barrier_semaphore()
    for d in range(1, 4):
        pl.semaphore_signal(barrier, inc=1, device_id=at_x(d), device_id_type=MESH)
        pl.semaphore_signal(barrier, inc=1, device_id=at_y(d), device_id_type=MESH)
    for d in range(1, 8):
        pl.semaphore_signal(barrier, inc=1, device_id=(lax.rem(row + d, 8), col), device_id_type=MESH)
    pl.semaphore_wait(barrier, 13)

    sends = []
    for d in (1, 3, 2):
        for h in range(2):
            u = d * 2 + h
            copy = pltpu.make_async_remote_copy(
                src_ref=piece(h, d), dst_ref=arrived.at[u], send_sem=s1.at[u], recv_sem=r1.at[u],
                device_id=ring(h, d), device_id_type=MESH)
            copy.start()
            sends.append(copy)

    tab_v[...] = slot_table(mu_ref[...], nu_ref[...])
    tab_r[0] = tab_v[...]
    tab_r[1] = tab_v[...]
    for d in (1, 3, 2):
        for h in range(2):
            u = d * 2 + h
            copy = pltpu.make_async_remote_copy(
                src_ref=tab_v, dst_ref=tab_r.at[u], send_sem=st.at[u], recv_sem=rt.at[u],
                device_id=ring(h, d), device_id_type=MESH)
            copy.start()
            sends.append(copy)
    occ[NBNU] = jnp.zeros((BS, NNU), BF16)
    for copy in sends[6:]:
        copy.wait_recv()
    tab_copy = pltpu.make_async_copy(tab_r, tab_s, tab_sem)
    tab_copy.start()
    c = lax.broadcasted_iota(jnp.int32, (128, 128), 1)
    r = lax.broadcasted_iota(jnp.int32, (128, 128), 0)
    from_col = (c // 64) * 64 + ((c // 32) % 2) * 32 + (c % 16) * 2 + (c // 16) % 2
    perm = jnp.where(r == from_col, 1.0, 0.0).astype(BF16)
    virt = jnp.dot(virt_ref[...], perm, preferred_element_type=F32).astype(BF16)
    tab_copy.wait()
    occ_copy.wait()

    def relayout(u, b):
        def body(i, _):
            a, tile = i // 4, lax.rem(i, 4)
            s0 = pl.multiple_of(tile * 16, 16)
            for ip in range(16):
                zbuf[pl.ds(ip * 16, 16), :] = arrived[u, a, pl.ds(s0, 16), pl.ds(ip * 128, 128)].astype(F32)
            for s in range(16):
                xt[b, s0 + s, pl.ds(pl.multiple_of(a * 16, 16), 16), :] = zbuf[pl.ds(s, 16, stride=16), :].astype(BF16)
            return 0
        lax.fori_loop(0, 16, body, 0)

    def product(u, b, m):
        even, odd, dens = [], [], []
        for q in range(0, CAPM, 2):
            t0 = xt[b, tab_s[u, 0, m * CAPM + q]]
            t1 = xt[b, tab_s[u, 0, m * CAPM + q + 1]]
            even.append(jnp.concatenate([t0[:, :64], t1[:, :64]], axis=1))
            odd.append(jnp.concatenate([t0[:, 64:], t1[:, 64:]], axis=1))
            dens.append(occ[tab_s[u, 1, m * CAPM + q]])
            dens.append(occ[tab_s[u, 1, m * CAPM + q + 1]])
        left = jnp.concatenate([jnp.concatenate(even, axis=1), jnp.concatenate(odd, axis=1)], axis=0)
        right = jnp.concatenate(dens, axis=0)
        return jnp.dot(left, right, preferred_element_type=F32)

    def store_sum(h, m, value, first):
        for ii in range(2):
            for a in range(4):
                part = value[(ii * 4 + a) * 16:(ii * 4 + a + 1) * 16]
                if first:
                    sums[h, m, ii, a] = part
                else:
                    sums[h, m, ii, a] += part

    for h in range(2):
        own[h].wait()
        relayout(h, 0)

        def first_body(m, _, h=h):
            store_sum(h, m, product(h, 0, m), True)
            return 0
        lax.fori_loop(0, NMB, first_body, 0)

    for d in (1, 3):
        for h in range(2):
            u = d * 2 + h
            sends[(0 if d == 1 else 2) + h].wait_recv()
            relayout(u, 0)

            def next_body(m, _, h=h, u=u):
                store_sum(h, m, product(u, 0, m), False)
                return 0
            lax.fori_loop(0, NMB, next_body, 0)

    for h in range(2):
        sends[4 + h].wait_recv()
        relayout(4 + h, h)

    second = {}
    for t in range(4):
        mu0 = lax.rem(z + ORDER[t], 4) * 4
        for h in range(2):
            me = y if h == 0 else x

            def last_body(i, _, h=h, t=t, mu0=mu0, me=me):
                m = mu0 + i
                store_sum(h, m, product(4 + h, h, m), False)
                for d in range(1, 4):
                    for ii in range(2):
                        sbuf[h, d - 1, t, i, ii] = sums[h, m, ii, lax.rem(me + d, 4)].astype(BF16)
                return 0
            lax.fori_loop(0, 4, last_body, 0)
            for d in (2, 1, 3):
                copy = pltpu.make_async_remote_copy(
                    src_ref=sbuf.at[h, d - 1, t], dst_ref=rbuf.at[h, d - 1, t],
                    send_sem=s2.at[h, d - 1, t], recv_sem=r2.at[h, d - 1, t],
                    device_id=ring(1 - h, d), device_id_type=MESH)
                copy.start()
                second[t, h, d] = copy

    third = {}
    for t in range(4):
        zt = lax.rem(z + ORDER[t], 4)
        mu0 = zt * 4
        for h in range(2):
            for d in (1, 3, 2):
                second[t, h, d].wait_recv()
            me = y if h == 0 else x
            for i in range(4):
                for ii in range(2):
                    total = sums[h, mu0 + i, ii, me]
                    for d in range(3):
                        total = total + rbuf[h, d, t, i, ii].astype(F32)
                    hbuf[t, i // 2, pl.ds(((i % 2) * 4 + h * 2 + ii) * 16, 16), :] = total.astype(BF16)
        if t < 3:
            for k in range(2):
                copy = pltpu.make_async_remote_copy(
                    src_ref=hbuf.at[t, k], dst_ref=gbuf.at[row],
                    send_sem=s3.at[t, k], recv_sem=r3.at[t, core],
                    device_id=(zt * 2 + k, col), device_id_type=MESH)
                copy.start()
                third[t, k] = copy
        else:
            copy = pltpu.make_async_remote_copy(
                src_ref=hbuf.at[t, 1 - core], dst_ref=gbuf.at[row],
                send_sem=s3.at[t, 0], recv_sem=r3.at[t, 0],
                device_id=(z * 2 + 1 - core, col), device_id_type=MESH)
            copy.start()
            third[t, 0] = copy
            mine = pltpu.make_async_copy(hbuf.at[t, core], gbuf.at[row], loc_sem)
            mine.start()

    for t in range(4):
        if t < 3:
            for k in range(2):
                g = lax.rem(z + 4 - ORDER[t], 4) * 2 + k
                pltpu.make_async_remote_copy(
                    src_ref=hbuf.at[t, k], dst_ref=gbuf.at[g], send_sem=s3.at[t, k], recv_sem=r3.at[t, k],
                    device_id=(zt * 2 + k, col), device_id_type=MESH).wait_recv()
                o_ref[g] = jnp.dot(virt, gbuf[g], preferred_element_type=F32).astype(BF16)
        else:
            mine.wait()
            o_ref[row] = jnp.dot(virt, gbuf[row], preferred_element_type=F32).astype(BF16)
            third[t, 0].wait_recv()
            g = z * 2 + 1 - core
            o_ref[g] = jnp.dot(virt, gbuf[g], preferred_element_type=F32).astype(BF16)

    for copy in sends + list(second.values()) + list(third.values()):
        copy.wait_send()


def local(tensor, pair_mu, pair_nu, occ_density, virt_density):
    dma = pltpu.SemaphoreType.DMA
    out = pl.pallas_call(
        kernel,
        out_shape=jax.ShapeDtypeStruct((8, 128, NNU), BF16),
        in_specs=[
            pl.BlockSpec(memory_space=pl.ANY),
            pl.BlockSpec(memory_space=pltpu.VMEM),
            pl.BlockSpec(memory_space=pltpu.VMEM),
            pl.BlockSpec(memory_space=pl.ANY),
            pl.BlockSpec(memory_space=pltpu.VMEM),
        ],
        out_specs=pl.BlockSpec(memory_space=pltpu.VMEM),
        scratch_shapes=[
            pltpu.VMEM((8, 4, PAIRS, HALF), BF16),
            pltpu.VMEM((NBNU + 1, BS, NNU), BF16),
            pltpu.VMEM((256, 128), F32),
            pltpu.VMEM((2, PAIRS, 64, 128), BF16),
            pltpu.VMEM((2, NMB, 2, 4, 16, NNU), F32),
            pltpu.VMEM((2, 3, 4, 4, 2, 16, NNU), BF16),
            pltpu.VMEM((2, 3, 4, 4, 2, 16, NNU), BF16),
            pltpu.VMEM((4, 2, 128, NNU), BF16),
            pltpu.VMEM((8, 128, NNU), BF16),
            pltpu.VMEM((8, 128), jnp.int32),
            pltpu.VMEM((8, 8, 128), jnp.int32),
            pltpu.SMEM((8, 8, 128), jnp.int32),
            dma, dma((2,)), dma((8,)), dma((8,)), dma((8,)), dma((8,)), dma,
            dma((2, 3, 4)), dma((2, 3, 4)), dma((4, 2)), dma((4, 2)), dma,
        ],
        compiler_params=pltpu.CompilerParams(
            collective_id=0, has_side_effects=True, vmem_limit_bytes=56 << 20),
        name="density_transform",
    )(
        tensor.reshape(4, 4, PAIRS, BS * BS),
        pair_mu.reshape(1, PAIRS),
        pair_nu.reshape(1, PAIRS),
        occ_density.reshape(NBNU, BS, NNU),
        virt_density,
    )
    return out.reshape(8, 1, 128, NNU)


def solution(mesh):
    placed = (P("row", "col", None), P("col"), P("col"), P(), P("row", None))
    return jax.shard_map(
        local, mesh=mesh, in_specs=placed, out_specs=P(None, "col", "row", None), check_vma=False
    )
```

```python
import jax
import jax.numpy as jnp
from jax import lax
from jax.experimental import pallas as pl
from jax.experimental.pallas import tpu as pltpu
from jax.sharding import PartitionSpec as P

MESH = pl.DeviceIdType.MESH
BS = 64
NNU = 384
NBNU = 128
NMB = 16
CAPM = 8
PAIRS = 64
HALF = 2048
F32 = jnp.float32
BF16 = jnp.bfloat16


def slot_table(mu_row, nu_row):
    sub = lax.broadcasted_iota(jnp.int32, (PAIRS, PAIRS), 0)
    lane = lax.broadcasted_iota(jnp.int32, (PAIRS, PAIRS), 1)
    mu_b = jnp.broadcast_to(mu_row, (PAIRS, PAIRS))
    nu_b = jnp.broadcast_to(nu_row, (PAIRS, PAIRS))
    mu_col = jnp.sum(jnp.where(sub == lane, mu_b, 0), axis=1, keepdims=True)
    nu_col = jnp.sum(jnp.where(sub == lane, nu_b, 0), axis=1, keepdims=True)
    rank = jnp.sum(jnp.where((mu_b == mu_col) & (lane < sub), 1, 0), axis=1, keepdims=True)
    slot = lax.broadcasted_iota(jnp.int32, (PAIRS, NMB * CAPM), 1)
    pair = lax.broadcasted_iota(jnp.int32, (PAIRS, NMB * CAPM), 0)
    hit = (mu_col * CAPM + rank) == slot
    source = jnp.sum(jnp.where(hit, pair, 0), axis=0, keepdims=True)
    target = jnp.sum(jnp.where(hit, nu_col - NBNU, 0), axis=0, keepdims=True) + NBNU
    row = lax.broadcasted_iota(jnp.int32, (8, NMB * CAPM), 0)
    return jnp.where(row == 0, source, target)


def kernel(t_ref, mu_ref, nu_ref, occ_ref, virt_ref, o_ref,
           own, arr_c, arr_d, occ, xown, xt, sums, csums, cbuf, crecv, tbuf, sbuf, rbuf, hbuf, gbuf, tab_v, tab_r, tab_s,
           occ_sem, own_sem, sc, rc, sd, rd, st, rt, tab_sem, sp, rp, s2, r2, s3, r3, loc_sem):
    row, col = lax.axis_index("row"), lax.axis_index("col")
    x, y, z, core = col // 4, col % 4, row // 2, row % 2

    def at_x(d):
        return (row, lax.rem(x + d, 4) * 4 + y)

    def at_y(d):
        return (row, x * 4 + lax.rem(y + d, 4))

    def ring(h, d):
        return at_x(d) if h == 0 else at_y(d)

    def place(h):
        return x if h == 0 else y

    def piece(h, d, first, count):
        if h == 0:
            return t_ref.at[lax.rem(x + d, 4), pl.ds(first, count), :, pl.ds(0, HALF)]
        return t_ref.at[pl.ds(first, count), lax.rem(y + d, 4), :, pl.ds(HALF, HALF)]

    locals_ = []
    for h in range(2):
        for k, (d, first, count, at) in enumerate(((0, 0, 4, 0), (1, 0, 2, 4), (3, 2, 2, 6))):
            copy = pltpu.make_async_copy(piece(h, d, first, count), own.at[h, pl.ds(at, count)], own_sem.at[h, k])
            copy.start()
            locals_.append(copy)
    occ_copy = pltpu.make_async_copy(occ_ref, occ.at[pl.ds(0, NBNU)], occ_sem)
    occ_copy.start()

    barrier = pltpu.get_barrier_semaphore()
    for d in range(1, 4):
        pl.semaphore_signal(barrier, inc=1, device_id=at_x(d), device_id_type=MESH)
        pl.semaphore_signal(barrier, inc=1, device_id=at_y(d), device_id_type=MESH)
    for d in range(1, 8):
        pl.semaphore_signal(barrier, inc=1, device_id=(lax.rem(row + d, 8), col), device_id_type=MESH)
    pl.semaphore_wait(barrier, 13)

    cs, ds, tabs = {}, {}, {}
    for w in range(2):
        for h in range(2):
            cs[h, w] = pltpu.make_async_remote_copy(
                src_ref=piece(h, 2, 2 * w, 2), dst_ref=arr_c.at[h * 2 + w], send_sem=sc.at[h, w], recv_sem=rc.at[h, w],
                device_id=ring(h, 1 + 2 * w), device_id_type=MESH)
            ds[h, w] = pltpu.make_async_remote_copy(
                src_ref=piece(h, 1 + 2 * w, 2 - 2 * w, 2), dst_ref=arr_d.at[h * 2 + w], send_sem=sd.at[h, w], recv_sem=rd.at[h, w],
                device_id=ring(h, 1 + 2 * w), device_id_type=MESH)
            cs[h, w].start()

    tab_v[...] = slot_table(mu_ref[...], nu_ref[...])
    tab_r[4] = tab_v[...]
    for w in range(2):
        for h in range(2):
            copy = pltpu.make_async_remote_copy(
                src_ref=tab_v, dst_ref=tab_r.at[h * 2 + w], send_sem=st.at[h, w], recv_sem=rt.at[h, w],
                device_id=ring(h, 1 + 2 * w), device_id_type=MESH)
            copy.start()
            tabs[h, w] = copy
    occ[NBNU] = jnp.zeros((BS, NNU), BF16)
    c = lax.broadcasted_iota(jnp.int32, (128, 128), 1)
    r = lax.broadcasted_iota(jnp.int32, (128, 128), 0)
    from_col = (c // 64) * 64 + ((c // 32) % 2) * 32 + (c % 16) * 2 + (c // 16) % 2
    perm = jnp.where(r == from_col, 1.0, 0.0).astype(BF16)
    virt = jnp.dot(virt_ref[...], perm, preferred_element_type=F32).astype(BF16)

    def relayout(src, dst, aux_count):
        def body(i, _):
            a, s0 = i // 4, pl.multiple_of(lax.rem(i, 4) * 16, 16)
            dst[pl.ds(s0, 16), pl.ds(pl.multiple_of(a * 16, 16), 16), :] = src[a, pl.ds(s0, 16), :].reshape(16, 16, 128)
            return 0
        lax.fori_loop(0, aux_count * 4, body, 0, unroll=2)

    for copy in locals_:
        copy.wait()
    for h in range(2):
        relayout(own.at[h], xown.at[h], 8)
    for copy in tabs.values():
        copy.wait_recv()
    tab_copy = pltpu.make_async_copy(tab_r, tab_s, tab_sem)
    tab_copy.start()
    tab_copy.wait()
    occ_copy.wait()

    def product(blocks, k, m):
        even, odd, dens = [], [], []
        for q in range(0, CAPM, 2):
            t0 = blocks[tab_s[k, 0, m * CAPM + q]]
            t1 = blocks[tab_s[k, 0, m * CAPM + q + 1]]
            even.append(jnp.concatenate([t0[:, :64], t1[:, :64]], axis=1))
            odd.append(jnp.concatenate([t0[:, 64:], t1[:, 64:]], axis=1))
            dens.append(occ[tab_s[k, 1, m * CAPM + q]])
            dens.append(occ[tab_s[k, 1, m * CAPM + q + 1]])
        left = jnp.concatenate([jnp.concatenate(even, axis=1), jnp.concatenate(odd, axis=1)], axis=0)
        right = jnp.concatenate(dens, axis=0)
        return jnp.dot(left, right, preferred_element_type=F32)

    def own_body(m, _):
        for h in range(2):
            value = product(xown.at[h], 4, m).reshape(2, 8, 16, NNU)
            sums[h, m] = value[:, 0:4]
            csums[h * 2, m] = value[:, 4:6]
            csums[h * 2 + 1, m] = value[:, 6:8]
        return 0
    lax.fori_loop(0, NMB, own_body, 0, unroll=2)

    for copy in cs.values():
        copy.wait_send()
    for copy in ds.values():
        copy.start()
    for u in range(4):
        cs[u // 2, u % 2].wait_recv()
        relayout(arr_c.at[u], xt.at[u], 2)

    def pair_copy(u, t):
        return pltpu.make_async_remote_copy(
            src_ref=cbuf.at[u, t], dst_ref=crecv.at[u, t], send_sem=sp.at[u, t], recv_sem=rp.at[u, t],
            device_id=ring(u // 2, 1 + 2 * (u % 2)), device_id_type=MESH)

    def c_body(t, _):
        mu0 = lax.rem(z + t + 1, 4) * 4
        for u in range(4):
            for i in range(4):
                value = product(xt.at[u], u, mu0 + i).reshape(2, 2, 16, NNU)
                cbuf[u, t, i] = (value + csums[u, mu0 + i]).astype(BF16)
        for u in range(4):
            pair_copy(u, t).start()
        return 0
    lax.fori_loop(0, 4, c_body, 0)

    for u in range(4):
        ds[u // 2, u % 2].wait_recv()
        relayout(arr_d.at[u], xt.at[u], 2)

    def d_body(m, _):
        for u in range(4):
            h, w = u // 2, u % 2
            value = product(xt.at[u], u, m).reshape(2, 2, 16, NNU)
            sums[h, m, :, pl.ds(2 - 2 * w, 2)] += value
        return 0
    lax.fori_loop(0, NMB, d_body, 0, unroll=2)

    def second(h, d, t):
        return pltpu.make_async_remote_copy(
            src_ref=sbuf.at[h, d - 1, t], dst_ref=rbuf.at[h, d - 1, t],
            send_sem=s2.at[h, d - 1, t], recv_sem=r2.at[h, d - 1, t],
            device_id=ring(1 - h, d), device_id_type=MESH)

    def p2_body(t, _):
        mu0 = lax.rem(z + t + 1, 4) * 4
        for h in range(2):
            for w in range(2):
                pair_copy(h * 2 + w, t).wait_recv()
            for d in (2, 1, 3, 0):
                a = lax.rem(place(1 - h) + d, 4)
                for i in range(4):
                    for ii in range(2):
                        total = sums[h, mu0 + i, ii, a] + crecv[h * 2 + a // 2, t, i, ii, lax.rem(a, 2)].astype(F32)
                        if d == 0:
                            tbuf[h, t, i, ii] = total
                        else:
                            sbuf[h, d - 1, t, i, ii] = total.astype(BF16)
                if d > 0:
                    second(h, d, t).start()
        return 0
    lax.fori_loop(0, 4, p2_body, 0)

    def third(t, k):
        return pltpu.make_async_remote_copy(
            src_ref=hbuf.at[t, k], dst_ref=gbuf.at[row],
            send_sem=s3.at[t, k], recv_sem=r3.at[t, core],
            device_id=(lax.rem(z + t + 1, 4) * 2 + k, col), device_id_type=MESH)

    across = pltpu.make_async_remote_copy(
        src_ref=hbuf.at[3, 1 - core], dst_ref=gbuf.at[row],
        send_sem=s3.at[3, 0], recv_sem=r3.at[3, 0],
        device_id=(z * 2 + 1 - core, col), device_id_type=MESH)
    mine = pltpu.make_async_copy(hbuf.at[3, core], gbuf.at[row], loc_sem)

    def finish(t):
        for h in range(2):
            for d in (1, 3, 2):
                second(h, d, t).wait_recv()
            for i in range(4):
                for ii in range(2):
                    total = tbuf[h, t, i, ii]
                    for d in range(3):
                        total = total + rbuf[h, d, t, i, ii].astype(F32)
                    hbuf[t, i // 2, pl.ds(((i % 2) * 4 + h * 2 + ii) * 16, 16), :] = total.astype(BF16)

    def p3_body(t, _):
        finish(t)
        for k in range(2):
            third(t, k).start()
        return 0
    lax.fori_loop(0, 3, p3_body, 0)
    finish(3)
    across.start()
    mine.start()

    def last_body(t, _):
        for k in range(2):
            g = lax.rem(z + 3 - t, 4) * 2 + k
            pltpu.make_async_remote_copy(
                src_ref=hbuf.at[t, k], dst_ref=gbuf.at[g], send_sem=s3.at[t, k], recv_sem=r3.at[t, k],
                device_id=(row, col), device_id_type=MESH).wait_recv()
            o_ref[g] = jnp.dot(virt, gbuf[g], preferred_element_type=F32).astype(BF16)
        return 0
    lax.fori_loop(0, 3, last_body, 0)
    mine.wait()
    o_ref[row] = jnp.dot(virt, gbuf[row], preferred_element_type=F32).astype(BF16)
    across.wait_recv()
    other = z * 2 + 1 - core
    o_ref[other] = jnp.dot(virt, gbuf[other], preferred_element_type=F32).astype(BF16)

    across.wait_send()
    for copy in [*ds.values(), *tabs.values()]:
        copy.wait_send()

    def sent_body(t, _):
        for u in range(4):
            pair_copy(u, t).wait_send()
        for h in range(2):
            for d in range(1, 4):
                second(h, d, t).wait_send()
        return 0
    lax.fori_loop(0, 4, sent_body, 0)
    for t in range(3):
        for k in range(2):
            third(t, k).wait_send()


def local(tensor, pair_mu, pair_nu, occ_density, virt_density):
    dma = pltpu.SemaphoreType.DMA
    out = pl.pallas_call(
        kernel,
        out_shape=jax.ShapeDtypeStruct((8, 128, NNU), BF16),
        in_specs=[
            pl.BlockSpec(memory_space=pl.ANY),
            pl.BlockSpec(memory_space=pltpu.VMEM),
            pl.BlockSpec(memory_space=pltpu.VMEM),
            pl.BlockSpec(memory_space=pl.ANY),
            pl.BlockSpec(memory_space=pltpu.VMEM),
        ],
        out_specs=pl.BlockSpec(memory_space=pltpu.VMEM),
        scratch_shapes=[
            pltpu.VMEM((2, 8, PAIRS, HALF), BF16),
            pltpu.VMEM((4, 2, PAIRS, HALF), BF16),
            pltpu.VMEM((4, 2, PAIRS, HALF), BF16),
            pltpu.VMEM((NBNU + 1, BS, NNU), BF16),
            pltpu.VMEM((2, PAIRS, 128, 128), BF16),
            pltpu.VMEM((4, PAIRS, 32, 128), BF16),
            pltpu.VMEM((2, NMB, 2, 4, 16, NNU), F32),
            pltpu.VMEM((4, NMB, 2, 2, 16, NNU), F32),
            pltpu.VMEM((4, 4, 4, 2, 2, 16, NNU), BF16),
            pltpu.VMEM((4, 4, 4, 2, 2, 16, NNU), BF16),
            pltpu.VMEM((2, 4, 4, 2, 16, NNU), F32),
            pltpu.VMEM((2, 3, 4, 4, 2, 16, NNU), BF16),
            pltpu.VMEM((2, 3, 4, 4, 2, 16, NNU), BF16),
            pltpu.VMEM((4, 2, 128, NNU), BF16),
            pltpu.VMEM((8, 128, NNU), BF16),
            pltpu.VMEM((8, 128), jnp.int32),
            pltpu.VMEM((5, 8, 128), jnp.int32),
            pltpu.SMEM((5, 8, 128), jnp.int32),
            dma, dma((2, 3)), dma((2, 2)), dma((2, 2)), dma((2, 2)), dma((2, 2)), dma((2, 2)), dma((2, 2)), dma,
            dma((4, 4)), dma((4, 4)), dma((2, 3, 4)), dma((2, 3, 4)), dma((4, 2)), dma((4, 2)), dma,
        ],
        compiler_params=pltpu.CompilerParams(
            collective_id=0, has_side_effects=True, vmem_limit_bytes=60 << 20),
        name="density_transform",
    )(
        tensor.reshape(4, 4, PAIRS, BS * BS),
        pair_mu.reshape(1, PAIRS),
        pair_nu.reshape(1, PAIRS),
        occ_density.reshape(NBNU, BS, NNU),
        virt_density,
    )
    return out.reshape(8, 1, 128, NNU)


def solution(mesh):
    placed = (P("row", "col", None), P("col"), P("col"), P(), P("row", None))
    return jax.shard_map(
        local, mesh=mesh, in_specs=placed, out_specs=P(None, "col", "row", None), check_vma=False
    )
```

```python
import jax
import jax.numpy as jnp
from jax import lax
from jax.experimental import pallas as pl
from jax.experimental.pallas import tpu as pltpu
from jax.sharding import PartitionSpec as P

MESH = pl.DeviceIdType.MESH
BS = 64
NNU = 384
NBNU = 128
NMB = 16
CAPM = 8
PAIRS = 64
CHUNKS = 8
EARLY = 1
AHEAD = 2
LAG = 2
HALF = 2048
F32 = jnp.float32
BF16 = jnp.bfloat16


def slot_table(mu_row, nu_row):
    sub = lax.broadcasted_iota(jnp.int32, (PAIRS, PAIRS), 0)
    lane = lax.broadcasted_iota(jnp.int32, (PAIRS, PAIRS), 1)
    mu_b = jnp.broadcast_to(mu_row, (PAIRS, PAIRS))
    nu_b = jnp.broadcast_to(nu_row, (PAIRS, PAIRS))
    mu_col = jnp.sum(jnp.where(sub == lane, mu_b, 0), axis=1, keepdims=True)
    nu_col = jnp.sum(jnp.where(sub == lane, nu_b, 0), axis=1, keepdims=True)
    rank = jnp.sum(jnp.where((mu_b == mu_col) & (lane < sub), 1, 0), axis=1, keepdims=True)
    slot = lax.broadcasted_iota(jnp.int32, (PAIRS, NMB * CAPM), 1)
    pair = lax.broadcasted_iota(jnp.int32, (PAIRS, NMB * CAPM), 0)
    hit = (mu_col * CAPM + rank) == slot
    source = jnp.sum(jnp.where(hit, pair, 0), axis=0, keepdims=True)
    target = jnp.sum(jnp.where(hit, nu_col - NBNU, 0), axis=0, keepdims=True) + NBNU
    row = lax.broadcasted_iota(jnp.int32, (8, NMB * CAPM), 0)
    return jnp.where(row == 0, source, target)


def kernel(t_ref, mu_ref, nu_ref, occ_ref, virt_ref, o_ref,
           own, arr_c, arr_d, occ, xown, xt, sums, csums, cbuf, crecv, tbuf, sbuf, rbuf, hbuf, gbuf, tab_v, tab_r, tab_s,
           occ_sem, own_sem, sc, rc, sd, rd, st, rt, tab_sem, sp, rp, s2, r2, s3, r3):
    row, col = lax.axis_index("row"), lax.axis_index("col")
    x, y, z, core = col // 4, col % 4, row // 2, row % 2

    def at_x(d):
        return (row, lax.rem(x + d, 4) * 4 + y)

    def at_y(d):
        return (row, x * 4 + lax.rem(y + d, 4))

    def ring(h, d):
        return at_x(d) if h == 0 else at_y(d)

    def place(h):
        return x if h == 0 else y

    def piece(h, d, first, count):
        if h == 0:
            return t_ref.at[lax.rem(x + d, 4), pl.ds(first, count), :, pl.ds(0, HALF)]
        return t_ref.at[pl.ds(first, count), lax.rem(y + d, 4), :, pl.ds(HALF, HALF)]

    locals_ = []
    for h in range(2):
        for k, (d, first, count, at) in enumerate(((0, 0, 4, 0), (1, 0, 2, 4), (3, 2, 2, 6))):
            copy = pltpu.make_async_copy(piece(h, d, first, count), own.at[h, pl.ds(at, count)], own_sem.at[h, k])
            copy.start()
            locals_.append(copy)
    occ_copy = pltpu.make_async_copy(occ_ref, occ.at[pl.ds(0, NBNU)], occ_sem)
    occ_copy.start()

    barrier = pltpu.get_barrier_semaphore()
    for d in range(1, 4):
        pl.semaphore_signal(barrier, inc=1, device_id=at_x(d), device_id_type=MESH)
        pl.semaphore_signal(barrier, inc=1, device_id=at_y(d), device_id_type=MESH)
    for d in range(1, 8):
        pl.semaphore_signal(barrier, inc=1, device_id=(lax.rem(row + d, 8), col), device_id_type=MESH)
    pl.semaphore_wait(barrier, 13)

    cs, ds, tabs = {}, {}, {}
    for w in range(2):
        for h in range(2):
            cs[h, w] = pltpu.make_async_remote_copy(
                src_ref=piece(h, 2, 2 * w, 2), dst_ref=arr_c.at[h * 2 + w], send_sem=sc.at[h, w], recv_sem=rc.at[h, w],
                device_id=ring(h, 1 + 2 * w), device_id_type=MESH)
            ds[h, w] = pltpu.make_async_remote_copy(
                src_ref=piece(h, 1 + 2 * w, 2 - 2 * w, 2), dst_ref=arr_d.at[h * 2 + w], send_sem=sd.at[h, w], recv_sem=rd.at[h, w],
                device_id=ring(h, 1 + 2 * w), device_id_type=MESH)
            cs[h, w].start()

    tab_v[...] = slot_table(mu_ref[...], nu_ref[...])
    tab_r[4] = tab_v[...]
    for w in range(2):
        for h in range(2):
            copy = pltpu.make_async_remote_copy(
                src_ref=tab_v, dst_ref=tab_r.at[h * 2 + w], send_sem=st.at[h, w], recv_sem=rt.at[h, w],
                device_id=ring(h, 1 + 2 * w), device_id_type=MESH)
            copy.start()
            tabs[h, w] = copy
    occ[NBNU] = jnp.zeros((BS, NNU), BF16)
    c = lax.broadcasted_iota(jnp.int32, (128, 128), 1)
    r = lax.broadcasted_iota(jnp.int32, (128, 128), 0)
    from_col = (c // 64) * 64 + ((c // 32) % 2) * 32 + (c % 16) * 2 + (c // 16) % 2
    perm = jnp.where(r == from_col, 1.0, 0.0).astype(BF16)
    virt = jnp.dot(virt_ref[...], perm, preferred_element_type=F32).astype(BF16)

    def relayout(src, dst, aux_count):
        def body(i, _):
            a, s0 = i // 4, pl.multiple_of(lax.rem(i, 4) * 16, 16)
            dst[pl.ds(s0, 16), pl.ds(pl.multiple_of(a * 16, 16), 16), :] = src[a, pl.ds(s0, 16), :].reshape(16, 16, 128)
            return 0
        lax.fori_loop(0, aux_count * 4, body, 0, unroll=2)

    for copy in locals_:
        copy.wait()
    for h in range(2):
        relayout(own.at[h], xown.at[h], 8)
    for copy in tabs.values():
        copy.wait_recv()
    tab_copy = pltpu.make_async_copy(tab_r, tab_s, tab_sem)
    tab_copy.start()
    tab_copy.wait()
    occ_copy.wait()

    def product(blocks, k, m):
        even, odd, dens = [], [], []
        for q in range(0, CAPM, 2):
            t0 = blocks[tab_s[k, 0, m * CAPM + q]]
            t1 = blocks[tab_s[k, 0, m * CAPM + q + 1]]
            even.append(jnp.concatenate([t0[:, :64], t1[:, :64]], axis=1))
            odd.append(jnp.concatenate([t0[:, 64:], t1[:, 64:]], axis=1))
            dens.append(occ[tab_s[k, 1, m * CAPM + q]])
            dens.append(occ[tab_s[k, 1, m * CAPM + q + 1]])
        left = jnp.concatenate([jnp.concatenate(even, axis=1), jnp.concatenate(odd, axis=1)], axis=0)
        right = jnp.concatenate(dens, axis=0)
        return jnp.dot(left, right, preferred_element_type=F32)

    def own_body(m, _):
        for h in range(2):
            value = product(xown.at[h], 4, m).reshape(2, 8, 16, NNU)
            sums[h, m] = value[:, 0:4]
            csums[h * 2, m] = value[:, 4:6]
            csums[h * 2 + 1, m] = value[:, 6:8]
        return 0
    lax.fori_loop(0, 4, own_body, 0, unroll=2)
    for copy in cs.values():
        copy.wait_send()
    for copy in ds.values():
        copy.start()
    lax.fori_loop(4, NMB, own_body, 0, unroll=2)

    for u in range(4):
        cs[u // 2, u % 2].wait_recv()
        relayout(arr_c.at[u], xt.at[u], 2)

    def chunk_row(t):
        return lax.rem(z + t // 2 + 1, 4) * 2 + lax.rem(t + 1 + core, 2)

    def pair_copy(u, t):
        return pltpu.make_async_remote_copy(
            src_ref=cbuf.at[u, t], dst_ref=crecv.at[u, t], send_sem=sp.at[u, t], recv_sem=rp.at[u, t],
            device_id=ring(u // 2, 1 + 2 * (u % 2)), device_id_type=MESH)

    def start_pair(t):
        for u in range(4):
            pair_copy(u, t).start()

    def c_body(t, _):
        mu0 = chunk_row(t) * 2
        for u in range(4):
            for i in range(2):
                value = product(xt.at[u], u, mu0 + i).reshape(2, 2, 16, NNU)
                cbuf[u, t, i] = (value + csums[u, mu0 + i]).astype(BF16)

        @pl.when(t < EARLY)
        def _():
            start_pair(t)
        return 0
    lax.fori_loop(0, CHUNKS, c_body, 0)

    for copy in ds.values():
        copy.wait_send()
    for t in range(EARLY, AHEAD):
        start_pair(t)
    for u in range(4):
        ds[u // 2, u % 2].wait_recv()
        relayout(arr_d.at[u], xt.at[u], 2)

    def direct(m):
        for u in range(4):
            h, w = u // 2, u % 2
            value = product(xt.at[u], u, m).reshape(2, 2, 16, NNU)
            sums[h, m, :, pl.ds(2 - 2 * w, 2)] += value

    def second(h, d, t):
        return pltpu.make_async_remote_copy(
            src_ref=sbuf.at[h, d - 1, t], dst_ref=rbuf.at[h, d - 1, t],
            send_sem=s2.at[h, d - 1, t], recv_sem=r2.at[h, d - 1, t],
            device_id=ring(1 - h, d), device_id_type=MESH)

    def third(t):
        return pltpu.make_async_remote_copy(
            src_ref=hbuf.at[t], dst_ref=gbuf.at[row], send_sem=s3.at[t], recv_sem=r3.at[t],
            device_id=(chunk_row(t), col), device_id_type=MESH)

    def finish(t):
        for h in range(2):
            for d in (1, 3, 2):
                second(h, d, t).wait_recv()
            for i in range(2):
                for ii in range(2):
                    total = tbuf[h, t, i, ii]
                    for d in range(3):
                        total = total + rbuf[h, d, t, i, ii].astype(F32)
                    hbuf[t, pl.ds((i * 4 + h * 2 + ii) * 16, 16), :] = total.astype(BF16)

    def chunk(t, _):
        mu0 = chunk_row(t) * 2
        for i in range(2):
            direct(mu0 + i)
        for h in range(2):
            for w in range(2):
                pair_copy(h * 2 + w, t).wait_recv()
            for d in (2, 1, 3, 0):
                a = lax.rem(place(1 - h) + d, 4)
                for i in range(2):
                    for ii in range(2):
                        total = sums[h, mu0 + i, ii, a] + crecv[h * 2 + a // 2, t, i, ii, lax.rem(a, 2)].astype(F32)
                        if d == 0:
                            tbuf[h, t, i, ii] = total
                        else:
                            sbuf[h, d - 1, t, i, ii] = total.astype(BF16)
                if d > 0:
                    second(h, d, t).start()

        @pl.when(t < CHUNKS - AHEAD)
        def _():
            start_pair(t + AHEAD)

        @pl.when(t >= LAG)
        def _():
            finish(t - LAG)
            third(t - LAG).start()
        return 0
    lax.fori_loop(0, CHUNKS, chunk, 0)

    for t in range(CHUNKS - LAG, 7):
        finish(t)
        third(t).start()

    def last_body(t, _):
        g = lax.rem(z + 3 - t // 2, 4) * 2 + lax.rem(t + 1 + core, 2)
        pltpu.make_async_remote_copy(
            src_ref=hbuf.at[t], dst_ref=gbuf.at[g], send_sem=s3.at[t], recv_sem=r3.at[t],
            device_id=(row, col), device_id_type=MESH).wait_recv()
        o_ref[g] = jnp.dot(virt, gbuf[g], preferred_element_type=F32).astype(BF16)
        return 0
    lax.fori_loop(0, 6, last_body, 0)
    finish(7)
    o_ref[row] = jnp.dot(virt, hbuf[7], preferred_element_type=F32).astype(BF16)
    last_body(6, 0)

    for copy in tabs.values():
        copy.wait_send()

    def sent_body(t, _):
        for u in range(4):
            pair_copy(u, t).wait_send()
        for h in range(2):
            for d in range(1, 4):
                second(h, d, t).wait_send()

        @pl.when(t < 7)
        def _():
            third(t).wait_send()
        return 0
    lax.fori_loop(0, CHUNKS, sent_body, 0)


def local(tensor, pair_mu, pair_nu, occ_density, virt_density):
    dma = pltpu.SemaphoreType.DMA
    out = pl.pallas_call(
        kernel,
        out_shape=jax.ShapeDtypeStruct((8, 128, NNU), BF16),
        in_specs=[
            pl.BlockSpec(memory_space=pl.ANY),
            pl.BlockSpec(memory_space=pltpu.VMEM),
            pl.BlockSpec(memory_space=pltpu.VMEM),
            pl.BlockSpec(memory_space=pl.ANY),
            pl.BlockSpec(memory_space=pltpu.VMEM),
        ],
        out_specs=pl.BlockSpec(memory_space=pltpu.VMEM),
        scratch_shapes=[
            pltpu.VMEM((2, 8, PAIRS, HALF), BF16),
            pltpu.VMEM((4, 2, PAIRS, HALF), BF16),
            pltpu.VMEM((4, 2, PAIRS, HALF), BF16),
            pltpu.VMEM((NBNU + 1, BS, NNU), BF16),
            pltpu.VMEM((2, PAIRS, 128, 128), BF16),
            pltpu.VMEM((4, PAIRS, 32, 128), BF16),
            pltpu.VMEM((2, NMB, 2, 4, 16, NNU), F32),
            pltpu.VMEM((4, NMB, 2, 2, 16, NNU), F32),
            pltpu.VMEM((4, CHUNKS, 2, 2, 2, 16, NNU), BF16),
            pltpu.VMEM((4, CHUNKS, 2, 2, 2, 16, NNU), BF16),
            pltpu.VMEM((2, CHUNKS, 2, 2, 16, NNU), F32),
            pltpu.VMEM((2, 3, CHUNKS, 2, 2, 16, NNU), BF16),
            pltpu.VMEM((2, 3, CHUNKS, 2, 2, 16, NNU), BF16),
            pltpu.VMEM((8, 128, NNU), BF16),
            pltpu.VMEM((8, 128, NNU), BF16),
            pltpu.VMEM((8, 128), jnp.int32),
            pltpu.VMEM((5, 8, 128), jnp.int32),
            pltpu.SMEM((5, 8, 128), jnp.int32),
            dma, dma((2, 3)), dma((2, 2)), dma((2, 2)), dma((2, 2)), dma((2, 2)), dma((2, 2)), dma((2, 2)), dma,
            dma((4, CHUNKS)), dma((4, CHUNKS)), dma((2, 3, CHUNKS)), dma((2, 3, CHUNKS)), dma((7,)), dma((7,)),
        ],
        compiler_params=pltpu.CompilerParams(
            collective_id=0, has_side_effects=True, vmem_limit_bytes=60 << 20),
        name="density_transform",
    )(
        tensor.reshape(4, 4, PAIRS, BS * BS),
        pair_mu.reshape(1, PAIRS),
        pair_nu.reshape(1, PAIRS),
        occ_density.reshape(NBNU, BS, NNU),
        virt_density,
    )
    return out.reshape(8, 1, 128, NNU)


def solution(mesh):
    placed = (P("row", "col", None), P("col"), P("col"), P(), P("row", None))
    return jax.shard_map(
        local, mesh=mesh, in_specs=placed, out_specs=P(None, "col", "row", None), check_vma=False
    )
```

```python
import jax
import jax.numpy as jnp
from jax import lax
from jax.experimental import pallas as pl
from jax.experimental.pallas import tpu as pltpu
from jax.sharding import PartitionSpec as P

MESH = pl.DeviceIdType.MESH
BS = 64
NNU = 384
NBNU = 128
NMB = 16
CAPM = 8
PAIRS = 64
CHUNKS = 8
EARLY = 3
AHEAD = 4
LAG = 3
HALF = 2048
F32 = jnp.float32
BF16 = jnp.bfloat16


def slot_table(mu_row, nu_row):
    sub = lax.broadcasted_iota(jnp.int32, (PAIRS, PAIRS), 0)
    lane = lax.broadcasted_iota(jnp.int32, (PAIRS, PAIRS), 1)
    mu_b = jnp.broadcast_to(mu_row, (PAIRS, PAIRS))
    nu_b = jnp.broadcast_to(nu_row, (PAIRS, PAIRS))
    mu_col = jnp.sum(jnp.where(sub == lane, mu_b, 0), axis=1, keepdims=True)
    nu_col = jnp.sum(jnp.where(sub == lane, nu_b, 0), axis=1, keepdims=True)
    rank = jnp.sum(jnp.where((mu_b == mu_col) & (lane < sub), 1, 0), axis=1, keepdims=True)
    slot = lax.broadcasted_iota(jnp.int32, (PAIRS, NMB * CAPM), 1)
    pair = lax.broadcasted_iota(jnp.int32, (PAIRS, NMB * CAPM), 0)
    hit = (mu_col * CAPM + rank) == slot
    source = jnp.sum(jnp.where(hit, pair, 0), axis=0, keepdims=True)
    target = jnp.sum(jnp.where(hit, nu_col - NBNU, 0), axis=0, keepdims=True) + NBNU
    row = lax.broadcasted_iota(jnp.int32, (8, NMB * CAPM), 0)
    return jnp.where(row == 0, source, target)


def kernel(t_ref, mu_ref, nu_ref, occ_ref, virt_ref, o_ref,
           own, arr_c, arr_d, occ, xown, xt, sums, csums, cbuf, crecv, tbuf, sbuf, rbuf, keep, gown, grecv, hbuf, gbuf, tab_v, tab_r, tab_s,
           occ_sem, own_sem, sc, rc, sd, rd, st, rt, tab_sem, sp, rp, s2, r2, sg, rg, s3, r3):
    row, col = lax.axis_index("row"), lax.axis_index("col")
    x, y, z, core = col // 4, col % 4, row // 2, row % 2

    def at_x(d):
        return (row, lax.rem(x + d, 4) * 4 + y)

    def at_y(d):
        return (row, x * 4 + lax.rem(y + d, 4))

    def ring(h, d):
        return at_x(d) if h == 0 else at_y(d)

    def place(h):
        return x if h == 0 else y

    def piece(h, d, first, count):
        if h == 0:
            return t_ref.at[lax.rem(x + d, 4), pl.ds(first, count), :, pl.ds(0, HALF)]
        return t_ref.at[pl.ds(first, count), lax.rem(y + d, 4), :, pl.ds(HALF, HALF)]

    locals_ = []
    for h in range(2):
        for k, (d, first, count, at) in enumerate(((0, 0, 4, 0), (1, 0, 2, 4), (3, 2, 2, 6))):
            copy = pltpu.make_async_copy(piece(h, d, first, count), own.at[h, pl.ds(at, count)], own_sem.at[h, k])
            copy.start()
            locals_.append(copy)
    occ_copy = pltpu.make_async_copy(occ_ref, occ.at[pl.ds(0, NBNU)], occ_sem)
    occ_copy.start()

    barrier = pltpu.get_barrier_semaphore()
    for d in range(1, 4):
        pl.semaphore_signal(barrier, inc=1, device_id=at_x(d), device_id_type=MESH)
        pl.semaphore_signal(barrier, inc=1, device_id=at_y(d), device_id_type=MESH)
    for d in range(1, 8):
        pl.semaphore_signal(barrier, inc=1, device_id=(lax.rem(row + d, 8), col), device_id_type=MESH)
    pl.semaphore_wait(barrier, 13)

    cs, ds, tabs = {}, {}, {}
    for w in range(2):
        for h in range(2):
            cs[h, w] = pltpu.make_async_remote_copy(
                src_ref=piece(h, 2, 2 * w, 2), dst_ref=arr_c.at[h * 2 + w], send_sem=sc.at[h, w], recv_sem=rc.at[h, w],
                device_id=ring(h, 1 + 2 * w), device_id_type=MESH)
            ds[h, w] = pltpu.make_async_remote_copy(
                src_ref=piece(h, 1 + 2 * w, 2 - 2 * w, 2), dst_ref=arr_d.at[h * 2 + w], send_sem=sd.at[h, w], recv_sem=rd.at[h, w],
                device_id=ring(h, 1 + 2 * w), device_id_type=MESH)
            cs[h, w].start()

    tab_v[...] = slot_table(mu_ref[...], nu_ref[...])
    tab_r[4] = tab_v[...]
    for w in range(2):
        for h in range(2):
            copy = pltpu.make_async_remote_copy(
                src_ref=tab_v, dst_ref=tab_r.at[h * 2 + w], send_sem=st.at[h, w], recv_sem=rt.at[h, w],
                device_id=ring(h, 1 + 2 * w), device_id_type=MESH)
            copy.start()
            tabs[h, w] = copy
    occ[NBNU] = jnp.zeros((BS, NNU), BF16)
    c = lax.broadcasted_iota(jnp.int32, (128, 128), 1)
    r = lax.broadcasted_iota(jnp.int32, (128, 128), 0)
    from_col = (c // 64) * 64 + ((c // 32) % 2) * 32 + (c % 16) * 2 + (c // 16) % 2
    perm = jnp.where(r == from_col, 1.0, 0.0).astype(BF16)
    virt = jnp.dot(virt_ref[...], perm, preferred_element_type=F32).astype(BF16)

    def relayout(src, dst, aux_count):
        def body(i, _):
            a, s0 = i // 4, pl.multiple_of(lax.rem(i, 4) * 16, 16)
            dst[pl.ds(s0, 16), pl.ds(pl.multiple_of(a * 16, 16), 16), :] = src[a, pl.ds(s0, 16), :].reshape(16, 16, 128)
            return 0
        lax.fori_loop(0, aux_count * 4, body, 0, unroll=2)

    for copy in locals_:
        copy.wait()
    for h in range(2):
        relayout(own.at[h], xown.at[h], 8)
    for copy in ds.values():
        copy.start()
    for copy in tabs.values():
        copy.wait_recv()
    tab_copy = pltpu.make_async_copy(tab_r, tab_s, tab_sem)
    tab_copy.start()
    tab_copy.wait()
    occ_copy.wait()

    def product(blocks, k, m):
        even, odd, dens = [], [], []
        for q in range(0, CAPM, 2):
            t0 = blocks[tab_s[k, 0, m * CAPM + q]]
            t1 = blocks[tab_s[k, 0, m * CAPM + q + 1]]
            even.append(jnp.concatenate([t0[:, :64], t1[:, :64]], axis=1))
            odd.append(jnp.concatenate([t0[:, 64:], t1[:, 64:]], axis=1))
            dens.append(occ[tab_s[k, 1, m * CAPM + q]])
            dens.append(occ[tab_s[k, 1, m * CAPM + q + 1]])
        left = jnp.concatenate([jnp.concatenate(even, axis=1), jnp.concatenate(odd, axis=1)], axis=0)
        right = jnp.concatenate(dens, axis=0)
        return jnp.dot(left, right, preferred_element_type=F32)

    def own_body(m, _):
        for h in range(2):
            value = product(xown.at[h], 4, m).reshape(2, 8, 16, NNU)
            sums[h, m] = value[:, 0:4]
            csums[h * 2, m] = value[:, 4:6]
            csums[h * 2 + 1, m] = value[:, 6:8]
        return 0
    lax.fori_loop(0, 4, own_body, 0, unroll=2)
    lax.fori_loop(4, NMB, own_body, 0, unroll=2)

    for u in range(4):
        cs[u // 2, u % 2].wait_recv()
        relayout(arr_c.at[u], xt.at[u], 2)

    def chunk_row(t):
        return lax.rem(z + t // 2 + 1, 4) * 2 + lax.rem(t + 1 + core, 2)

    def pair_copy(u, t):
        return pltpu.make_async_remote_copy(
            src_ref=cbuf.at[u, t], dst_ref=crecv.at[u, t], send_sem=sp.at[u, t], recv_sem=rp.at[u, t],
            device_id=ring(u // 2, 1 + 2 * (u % 2)), device_id_type=MESH)

    def start_pair(t):
        for u in range(4):
            pair_copy(u, t).start()

    def c_body(t, _):
        mu0 = chunk_row(t) * 2
        for u in range(4):
            for i in range(2):
                value = product(xt.at[u], u, mu0 + i).reshape(2, 2, 16, NNU)
                cbuf[u, t, i] = (value + csums[u, mu0 + i]).astype(BF16)

        @pl.when(t < EARLY)
        def _():
            start_pair(t)
        return 0
    lax.fori_loop(0, CHUNKS, c_body, 0)

    for copy in ds.values():
        copy.wait_send()
    for t in range(EARLY, AHEAD):
        start_pair(t)
    for u in range(4):
        ds[u // 2, u % 2].wait_recv()
        relayout(arr_d.at[u], xt.at[u], 2)

    def direct(m):
        for u in range(4):
            h, w = u // 2, u % 2
            value = product(xt.at[u], u, m).reshape(2, 2, 16, NNU)
            sums[h, m, :, pl.ds(2 - 2 * w, 2)] += value

    def outer(h, w, t):
        return pltpu.make_async_remote_copy(
            src_ref=sbuf.at[h, w, t], dst_ref=rbuf.at[h, w, t], send_sem=s2.at[h, w, t], recv_sem=r2.at[h, w, t],
            device_id=ring(1 - h, 1 + 2 * w), device_id_type=MESH)

    def inner(h, w, t):
        return pltpu.make_async_remote_copy(
            src_ref=gown.at[h, w, t], dst_ref=grecv.at[h, w, t], send_sem=sg.at[h, w, t], recv_sem=rg.at[h, w, t],
            device_id=ring(1 - h, 1 + 2 * w), device_id_type=MESH)

    def third(t):
        return pltpu.make_async_remote_copy(
            src_ref=hbuf.at[t], dst_ref=gbuf.at[row], send_sem=s3.at[t], recv_sem=r3.at[t],
            device_id=(chunk_row(t), col), device_id_type=MESH)

    def forward(t):
        for h in range(2):
            for w in range(2):
                outer(h, w, t).wait_recv()
                gown[h, w, t] = (keep[h, w, t] + rbuf[h, w, t, 0].astype(F32)).astype(BF16)
                inner(h, w, t).start()

    def finish(t):
        for h in range(2):
            for w in range(2):
                inner(h, w, t).wait_recv()
            for i in range(2):
                total = tbuf[h, t, i] + grecv[h, i, t].astype(F32) + rbuf[h, 1 - i, t, 1].astype(F32)
                hbuf[t, pl.ds((i * 2 + h) * 32, 32), :] = total.reshape(32, NNU).astype(BF16)

    def chunk(t, _):
        mu0 = chunk_row(t) * 2
        for i in range(2):
            direct(mu0 + i)
        for h in range(2):
            for w in range(2):
                pair_copy(h * 2 + w, t).wait_recv()

            def total(d, i, h=h):
                a = lax.rem(place(1 - h) + d, 4)
                return sums[h, mu0 + i, :, a] + crecv[h * 2 + a // 2, t, i, :, lax.rem(a, 2)].astype(F32)
            for w in range(2):
                sbuf[h, w, t, 0] = total(2, w).astype(BF16)
                sbuf[h, w, t, 1] = total(1 + 2 * w, 1 - w).astype(BF16)
                outer(h, w, t).start()
            for w in range(2):
                keep[h, w, t] = total(1 + 2 * w, w)
            for i in range(2):
                tbuf[h, t, i] = total(0, i)

        @pl.when(t < CHUNKS - AHEAD)
        def _():
            start_pair(t + AHEAD)

        @pl.when(t >= 1)
        def _():
            forward(t - 1)

        @pl.when(t >= LAG)
        def _():
            finish(t - LAG)
            third(t - LAG).start()
        return 0
    lax.fori_loop(0, CHUNKS, chunk, 0)
    forward(CHUNKS - 1)

    for t in range(CHUNKS - LAG, 7):
        finish(t)
        third(t).start()

    def last_body(t, _):
        g = lax.rem(z + 3 - t // 2, 4) * 2 + lax.rem(t + 1 + core, 2)
        pltpu.make_async_remote_copy(
            src_ref=hbuf.at[t], dst_ref=gbuf.at[g], send_sem=s3.at[t], recv_sem=r3.at[t],
            device_id=(row, col), device_id_type=MESH).wait_recv()
        o_ref[g] = jnp.dot(virt, gbuf[g], preferred_element_type=F32).astype(BF16)
        return 0
    lax.fori_loop(0, 6, last_body, 0)
    finish(7)
    o_ref[row] = jnp.dot(virt, hbuf[7], preferred_element_type=F32).astype(BF16)
    last_body(6, 0)

    for copy in [*cs.values(), *tabs.values()]:
        copy.wait_send()

    def sent_body(t, _):
        for u in range(4):
            pair_copy(u, t).wait_send()
        for h in range(2):
            for w in range(2):
                outer(h, w, t).wait_send()
                inner(h, w, t).wait_send()

        @pl.when(t < 7)
        def _():
            third(t).wait_send()
        return 0
    lax.fori_loop(0, CHUNKS, sent_body, 0)


def local(tensor, pair_mu, pair_nu, occ_density, virt_density):
    dma = pltpu.SemaphoreType.DMA
    out = pl.pallas_call(
        kernel,
        out_shape=jax.ShapeDtypeStruct((8, 128, NNU), BF16),
        in_specs=[
            pl.BlockSpec(memory_space=pl.ANY),
            pl.BlockSpec(memory_space=pltpu.VMEM),
            pl.BlockSpec(memory_space=pltpu.VMEM),
            pl.BlockSpec(memory_space=pl.ANY),
            pl.BlockSpec(memory_space=pltpu.VMEM),
        ],
        out_specs=pl.BlockSpec(memory_space=pltpu.VMEM),
        scratch_shapes=[
            pltpu.VMEM((2, 8, PAIRS, HALF), BF16),
            pltpu.VMEM((4, 2, PAIRS, HALF), BF16),
            pltpu.VMEM((4, 2, PAIRS, HALF), BF16),
            pltpu.VMEM((NBNU + 1, BS, NNU), BF16),
            pltpu.VMEM((2, PAIRS, 128, 128), BF16),
            pltpu.VMEM((4, PAIRS, 32, 128), BF16),
            pltpu.VMEM((2, NMB, 2, 4, 16, NNU), F32),
            pltpu.VMEM((4, NMB, 2, 2, 16, NNU), F32),
            pltpu.VMEM((4, CHUNKS, 2, 2, 2, 16, NNU), BF16),
            pltpu.VMEM((4, CHUNKS, 2, 2, 2, 16, NNU), BF16),
            pltpu.VMEM((2, CHUNKS, 2, 2, 16, NNU), F32),
            pltpu.VMEM((2, 2, CHUNKS, 2, 2, 16, NNU), BF16),
            pltpu.VMEM((2, 2, CHUNKS, 2, 2, 16, NNU), BF16),
            pltpu.VMEM((2, 2, CHUNKS, 2, 16, NNU), F32),
            pltpu.VMEM((2, 2, CHUNKS, 2, 16, NNU), BF16),
            pltpu.VMEM((2, 2, CHUNKS, 2, 16, NNU), BF16),
            pltpu.VMEM((8, 128, NNU), BF16),
            pltpu.VMEM((8, 128, NNU), BF16),
            pltpu.VMEM((8, 128), jnp.int32),
            pltpu.VMEM((5, 8, 128), jnp.int32),
            pltpu.SMEM((5, 8, 128), jnp.int32),
            dma, dma((2, 3)), dma((2, 2)), dma((2, 2)), dma((2, 2)), dma((2, 2)), dma((2, 2)), dma((2, 2)), dma,
            dma((4, CHUNKS)), dma((4, CHUNKS)), dma((2, 2, CHUNKS)), dma((2, 2, CHUNKS)),
            dma((2, 2, CHUNKS)), dma((2, 2, CHUNKS)), dma((7,)), dma((7,)),
        ],
        compiler_params=pltpu.CompilerParams(
            collective_id=0, has_side_effects=True, vmem_limit_bytes=60 << 20),
        name="density_transform",
    )(
        tensor.reshape(4, 4, PAIRS, BS * BS),
        pair_mu.reshape(1, PAIRS),
        pair_nu.reshape(1, PAIRS),
        occ_density.reshape(NBNU, BS, NNU),
        virt_density,
    )
    return out.reshape(8, 1, 128, NNU)


def solution(mesh):
    placed = (P("row", "col", None), P("col"), P("col"), P(), P("row", None))
    return jax.shard_map(
        local, mesh=mesh, in_specs=placed, out_specs=P(None, "col", "row", None), check_vma=False
    )
```

```python
import jax
import jax.numpy as jnp
from jax import lax
from jax.experimental import pallas as pl
from jax.experimental.pallas import tpu as pltpu
from jax.sharding import PartitionSpec as P

MESH = pl.DeviceIdType.MESH
BS = 64
NNU = 384
NBNU = 128
NMB = 16
CAPM = 8
PAIRS = 64
CHUNKS = 8
EARLY = 3
AHEAD = 3
LAG = 3
HALF = 2048
F32 = jnp.float32
BF16 = jnp.bfloat16


def slot_table(mu_row, nu_row):
    sub = lax.broadcasted_iota(jnp.int32, (PAIRS, PAIRS), 0)
    lane = lax.broadcasted_iota(jnp.int32, (PAIRS, PAIRS), 1)
    mu_b = jnp.broadcast_to(mu_row, (PAIRS, PAIRS))
    nu_b = jnp.broadcast_to(nu_row, (PAIRS, PAIRS))
    mu_col = jnp.sum(jnp.where(sub == lane, mu_b, 0), axis=1, keepdims=True)
    nu_col = jnp.sum(jnp.where(sub == lane, nu_b, 0), axis=1, keepdims=True)
    rank = jnp.sum(jnp.where((mu_b == mu_col) & (lane < sub), 1, 0), axis=1, keepdims=True)
    slot = lax.broadcasted_iota(jnp.int32, (PAIRS, NMB * CAPM), 1)
    pair = lax.broadcasted_iota(jnp.int32, (PAIRS, NMB * CAPM), 0)
    hit = (mu_col * CAPM + rank) == slot
    source = jnp.sum(jnp.where(hit, pair, 0), axis=0, keepdims=True)
    target = jnp.sum(jnp.where(hit, nu_col - NBNU, 0), axis=0, keepdims=True) + NBNU
    row = lax.broadcasted_iota(jnp.int32, (8, NMB * CAPM), 0)
    return jnp.where(row == 0, source, target)


def kernel(t_ref, mu_hbm, nu_hbm, occ_ref, virt_hbm, out_ref,
           mu_ref, nu_ref, virt_ref, o_ref, own, arr_c, arr_d, occ, xown, xt, sums, csums, cbuf, crecv, tbuf, sbuf, rbuf, keep, gown, grecv, hbuf, gbuf, tab_v, tab_r, tab_s,
           occ_sem, own_sem, sc, rc, sd, rd, st, rt, tab_sem, sp, rp, s2, r2, sg, rg, s3, r3, sl, rl, small_sem, out_sem):
    row, col = lax.axis_index("row"), lax.axis_index("col")
    x, y, z, core = col // 4, col % 4, row // 2, row % 2

    def at_x(d):
        return (row, lax.rem(x + d, 4) * 4 + y)

    def at_y(d):
        return (row, x * 4 + lax.rem(y + d, 4))

    def ring(h, d):
        return at_x(d) if h == 0 else at_y(d)

    def place(h):
        return x if h == 0 else y

    def piece(h, d, first, count):
        if h == 0:
            return t_ref.at[lax.rem(x + d, 4), pl.ds(first, count), :, pl.ds(0, HALF)]
        return t_ref.at[pl.ds(first, count), lax.rem(y + d, 4), :, pl.ds(HALF, HALF)]

    barrier = pltpu.get_barrier_semaphore()
    for d in range(1, 4):
        pl.semaphore_signal(barrier, inc=1, device_id=at_x(d), device_id_type=MESH)
        pl.semaphore_signal(barrier, inc=1, device_id=at_y(d), device_id_type=MESH)
    for d in range(1, 8):
        pl.semaphore_signal(barrier, inc=1, device_id=(lax.rem(row + d, 8), col), device_id_type=MESH)

    small = []
    for k, (src, dst) in enumerate(((mu_hbm, mu_ref), (nu_hbm, nu_ref), (virt_hbm, virt_ref))):
        copy = pltpu.make_async_copy(src, dst, small_sem.at[k])
        copy.start()
        small.append(copy)
    locals_ = []
    for h in range(2):
        for k, (d, first, count, at) in enumerate(((0, 0, 4, 0), (1, 0, 2, 4), (3, 2, 2, 6))):
            copy = pltpu.make_async_copy(piece(h, d, first, count), own.at[h, pl.ds(at, count)], own_sem.at[h, k])
            copy.start()
            locals_.append(copy)
    occ_copy = pltpu.make_async_copy(occ_ref, occ.at[pl.ds(0, NBNU)], occ_sem)
    occ_copy.start()

    pl.semaphore_wait(barrier, 13)

    cs, ds, tabs = {}, {}, {}
    for w in range(2):
        for h in range(2):
            cs[h, w] = pltpu.make_async_remote_copy(
                src_ref=piece(h, 2, 2 * w, 2), dst_ref=arr_c.at[h * 2 + w], send_sem=sc.at[h, w], recv_sem=rc.at[h, w],
                device_id=ring(h, 1 + 2 * w), device_id_type=MESH)
            ds[h, w] = pltpu.make_async_remote_copy(
                src_ref=piece(h, 1 + 2 * w, 2 - 2 * w, 2), dst_ref=arr_d.at[h * 2 + w], send_sem=sd.at[h, w], recv_sem=rd.at[h, w],
                device_id=ring(h, 1 + 2 * w), device_id_type=MESH)
            cs[h, w].start()

    for copy in small:
        copy.wait()
    tab_v[...] = slot_table(mu_ref[...], nu_ref[...])
    tab_r[4] = tab_v[...]
    for w in range(2):
        for h in range(2):
            copy = pltpu.make_async_remote_copy(
                src_ref=tab_v, dst_ref=tab_r.at[h * 2 + w], send_sem=st.at[h, w], recv_sem=rt.at[h, w],
                device_id=ring(h, 1 + 2 * w), device_id_type=MESH)
            copy.start()
            tabs[h, w] = copy
    occ[NBNU] = jnp.zeros((BS, NNU), BF16)
    c = lax.broadcasted_iota(jnp.int32, (128, 128), 1)
    r = lax.broadcasted_iota(jnp.int32, (128, 128), 0)
    from_col = (c // 64) * 64 + ((c // 32) % 2) * 32 + (c % 16) * 2 + (c // 16) % 2
    perm = jnp.where(r == from_col, 1.0, 0.0).astype(BF16)
    virt = jnp.dot(virt_ref[...], perm, preferred_element_type=F32).astype(BF16)

    def relayout(src, dst, aux_count):
        def body(i, _):
            a, s0 = i // 4, pl.multiple_of(lax.rem(i, 4) * 16, 16)
            dst[pl.ds(s0, 16), pl.ds(pl.multiple_of(a * 16, 16), 16), :] = src[a, pl.ds(s0, 16), :].reshape(16, 16, 128)
            return 0
        lax.fori_loop(0, aux_count * 4, body, 0, unroll=2)

    for copy in locals_:
        copy.wait()
    for h in range(2):
        relayout(own.at[h], xown.at[h], 8)
    for copy in ds.values():
        copy.start()
    for copy in tabs.values():
        copy.wait_recv()
    tab_copy = pltpu.make_async_copy(tab_r, tab_s, tab_sem)
    tab_copy.start()
    tab_copy.wait()
    occ_copy.wait()

    def product(blocks, k, m):
        even, odd, dens = [], [], []
        for q in range(0, CAPM, 2):
            t0 = blocks[tab_s[k, 0, m * CAPM + q]]
            t1 = blocks[tab_s[k, 0, m * CAPM + q + 1]]
            even.append(jnp.concatenate([t0[:, :64], t1[:, :64]], axis=1))
            odd.append(jnp.concatenate([t0[:, 64:], t1[:, 64:]], axis=1))
            dens.append(occ[tab_s[k, 1, m * CAPM + q]])
            dens.append(occ[tab_s[k, 1, m * CAPM + q + 1]])
        left = jnp.concatenate([jnp.concatenate(even, axis=1), jnp.concatenate(odd, axis=1)], axis=0)
        right = jnp.concatenate(dens, axis=0)
        return jnp.dot(left, right, preferred_element_type=F32)

    def own_body(m, _):
        for h in range(2):
            value = product(xown.at[h], 4, m).reshape(2, 8, 16, NNU)
            sums[h, m] = value[:, 0:4]
            csums[h * 2, m] = value[:, 4:6]
            csums[h * 2 + 1, m] = value[:, 6:8]
        return 0
    lax.fori_loop(0, 4, own_body, 0, unroll=2)
    lax.fori_loop(4, NMB, own_body, 0, unroll=2)

    for u in range(4):
        cs[u // 2, u % 2].wait_recv()
        relayout(arr_c.at[u], xt.at[u], 2)

    def chunk_row(t):
        return lax.rem(z + t // 2 + 1, 4) * 2 + lax.rem(t + 1 + core, 2)

    def pair_copy(u, t):
        return pltpu.make_async_remote_copy(
            src_ref=cbuf.at[u, t], dst_ref=crecv.at[u, t], send_sem=sp.at[u, t], recv_sem=rp.at[u, t],
            device_id=ring(u // 2, 1 + 2 * (u % 2)), device_id_type=MESH)

    def start_pair(t):
        for u in range(4):
            pair_copy(u, t).start()

    def c_body(t, _):
        mu0 = chunk_row(t) * 2
        for u in range(4):
            for i in range(2):
                value = product(xt.at[u], u, mu0 + i).reshape(2, 2, 16, NNU)
                cbuf[u, t, i] = (value + csums[u, mu0 + i]).astype(BF16)

        @pl.when(t < EARLY)
        def _():
            start_pair(t)
        return 0
    lax.fori_loop(0, CHUNKS, c_body, 0)

    for copy in ds.values():
        copy.wait_send()
    for t in range(EARLY, AHEAD):
        start_pair(t)
    for copy in [*cs.values(), *tabs.values()]:
        copy.wait_send()
    for u in range(4):
        ds[u // 2, u % 2].wait_recv()
        relayout(arr_d.at[u], xt.at[u], 2)

    def direct(m):
        for u in range(4):
            h, w = u // 2, u % 2
            value = product(xt.at[u], u, m).reshape(2, 2, 16, NNU)
            sums[h, m, :, pl.ds(2 - 2 * w, 2)] += value

    def outer(h, w, t):
        return pltpu.make_async_remote_copy(
            src_ref=sbuf.at[h, w, t], dst_ref=rbuf.at[h, w, t], send_sem=s2.at[h, w, t], recv_sem=r2.at[h, w, t],
            device_id=ring(1 - h, 1 + 2 * w), device_id_type=MESH)

    def inner(h, w, t):
        return pltpu.make_async_remote_copy(
            src_ref=gown.at[h, w, t], dst_ref=grecv.at[h, w, t], send_sem=sg.at[h, w, t], recv_sem=rg.at[h, w, t],
            device_id=ring(1 - h, 1 + 2 * w), device_id_type=MESH)

    LAST = CHUNKS - 1

    def straight(h, w, k):
        return pltpu.make_async_remote_copy(
            src_ref=sbuf.at[h, w, LAST, k], dst_ref=rbuf.at[h, w, LAST, k], send_sem=sl.at[h, w, k], recv_sem=rl.at[h, w, k],
            device_id=ring(1 - h, 2 if k == 0 else 1 + 2 * w), device_id_type=MESH)

    def third(t):
        return pltpu.make_async_remote_copy(
            src_ref=hbuf.at[t], dst_ref=gbuf.at[row], send_sem=s3.at[t], recv_sem=r3.at[t],
            device_id=(chunk_row(t), col), device_id_type=MESH)

    def forward(t):
        for h in range(2):
            for w in range(2):
                outer(h, w, t).wait()
                gown[h, w, t] = (keep[h, w, t] + rbuf[h, w, t, 0].astype(F32)).astype(BF16)
                inner(h, w, t).start()

    def finish(t, last=False):
        for h in range(2):
            for w in range(2):
                inner(h, w, t).wait()
                if last:
                    for k in range(2):
                        straight(h, w, k).wait()
            for i in range(2):
                total = tbuf[h, t, i] + grecv[h, i, t].astype(F32) + rbuf[h, 1 - i, t, 1].astype(F32)
                if last:
                    total = total + rbuf[h, i, t, 0].astype(F32)
                hbuf[t, pl.ds((i * 2 + h) * 32, 32), :] = total.reshape(32, NNU).astype(BF16)

    def chunk(t, last):
        mu0 = chunk_row(t) * 2
        for i in range(2):
            direct(mu0 + i)
        for h in range(2):
            for w in range(2):
                pair_copy(h * 2 + w, t).wait()

            def total(d, i, h=h):
                a = lax.rem(place(1 - h) + d, 4)
                return sums[h, mu0 + i, :, a] + crecv[h * 2 + a // 2, t, i, :, lax.rem(a, 2)].astype(F32)
            for w in range(2):
                sbuf[h, w, t, 0] = total(2, w).astype(BF16)
                sbuf[h, w, t, 1] = total(1 + 2 * w, 1 - w).astype(BF16)
                if last:
                    for k in range(2):
                        straight(h, w, k).start()
                else:
                    outer(h, w, t).start()
            for w in range(2):
                if last:
                    gown[h, w, t] = total(1 + 2 * w, w).astype(BF16)
                    inner(h, w, t).start()
                else:
                    keep[h, w, t] = total(1 + 2 * w, w)
            for i in range(2):
                tbuf[h, t, i] = total(0, i)

    def chunk_body(t, _):
        chunk(t, False)

        @pl.when(t < CHUNKS - AHEAD)
        def _():
            start_pair(t + AHEAD)

        @pl.when(t >= 1)
        def _():
            forward(t - 1)

        @pl.when(t >= LAG)
        def _():
            finish(t - LAG)
            third(t - LAG).start()
        return 0
    lax.fori_loop(0, LAST, chunk_body, 0)
    chunk(LAST, True)
    forward(LAST - 1)
    for t in range(LAST - LAG, LAST):
        finish(t)
        third(t).start()

    def out_copy(g):
        return pltpu.make_async_copy(o_ref.at[g], out_ref.at[g], out_sem.at[g])

    def emit(g, half):
        o_ref[g] = jnp.dot(virt, half, preferred_element_type=F32).astype(BF16)
        out_copy(g).start()

    def last_body(t, _):
        g = lax.rem(z + 3 - t // 2, 4) * 2 + lax.rem(t + 1 + core, 2)
        third(t).wait_send()
        pltpu.make_async_remote_copy(
            src_ref=hbuf.at[t], dst_ref=gbuf.at[g], send_sem=s3.at[t], recv_sem=r3.at[t],
            device_id=(row, col), device_id_type=MESH).wait_recv()
        emit(g, gbuf[g])
        return 0
    lax.fori_loop(0, 6, last_body, 0)
    last_body(6, 0)
    finish(LAST, True)
    emit(row, hbuf[LAST])
    for g in range(8):
        out_copy(g).wait()


def local(tensor, pair_mu, pair_nu, occ_density, virt_density):
    dma = pltpu.SemaphoreType.DMA
    out = pl.pallas_call(
        kernel,
        out_shape=jax.ShapeDtypeStruct((8, 128, NNU), BF16),
        in_specs=[
            pl.BlockSpec(memory_space=pl.ANY),
        ] * 5,
        out_specs=pl.BlockSpec(memory_space=pl.ANY),
        scratch_shapes=[
            pltpu.VMEM((1, PAIRS), jnp.int32),
            pltpu.VMEM((1, PAIRS), jnp.int32),
            pltpu.VMEM((128, 128), BF16),
            pltpu.VMEM((8, 128, NNU), BF16),
            pltpu.VMEM((2, 8, PAIRS, HALF), BF16),
            pltpu.VMEM((4, 2, PAIRS, HALF), BF16),
            pltpu.VMEM((4, 2, PAIRS, HALF), BF16),
            pltpu.VMEM((NBNU + 1, BS, NNU), BF16),
            pltpu.VMEM((2, PAIRS, 128, 128), BF16),
            pltpu.VMEM((4, PAIRS, 32, 128), BF16),
            pltpu.VMEM((2, NMB, 2, 4, 16, NNU), F32),
            pltpu.VMEM((4, NMB, 2, 2, 16, NNU), F32),
            pltpu.VMEM((4, CHUNKS, 2, 2, 2, 16, NNU), BF16),
            pltpu.VMEM((4, CHUNKS, 2, 2, 2, 16, NNU), BF16),
            pltpu.VMEM((2, CHUNKS, 2, 2, 16, NNU), F32),
            pltpu.VMEM((2, 2, CHUNKS, 2, 2, 16, NNU), BF16),
            pltpu.VMEM((2, 2, CHUNKS, 2, 2, 16, NNU), BF16),
            pltpu.VMEM((2, 2, CHUNKS, 2, 16, NNU), F32),
            pltpu.VMEM((2, 2, CHUNKS, 2, 16, NNU), BF16),
            pltpu.VMEM((2, 2, CHUNKS, 2, 16, NNU), BF16),
            pltpu.VMEM((8, 128, NNU), BF16),
            pltpu.VMEM((8, 128, NNU), BF16),
            pltpu.VMEM((8, 128), jnp.int32),
            pltpu.VMEM((5, 8, 128), jnp.int32),
            pltpu.SMEM((5, 8, 128), jnp.int32),
            dma, dma((2, 3)), dma((2, 2)), dma((2, 2)), dma((2, 2)), dma((2, 2)), dma((2, 2)), dma((2, 2)), dma,
            dma((4, CHUNKS)), dma((4, CHUNKS)), dma((2, 2, CHUNKS)), dma((2, 2, CHUNKS)),
            dma((2, 2, CHUNKS)), dma((2, 2, CHUNKS)), dma((7,)), dma((7,)), dma((2, 2, 2)), dma((2, 2, 2)),
            dma((3,)), dma((8,)),
        ],
        compiler_params=pltpu.CompilerParams(
            collective_id=0, has_side_effects=True, vmem_limit_bytes=60 << 20),
        name="density_transform",
    )(
        tensor.reshape(4, 4, PAIRS, BS * BS),
        pair_mu.reshape(1, PAIRS),
        pair_nu.reshape(1, PAIRS),
        occ_density.reshape(NBNU, BS, NNU),
        virt_density,
    )
    return out.reshape(8, 1, 128, NNU)


def solution(mesh):
    placed = (P("row", "col", None), P("col"), P("col"), P(), P("row", None))
    return jax.shard_map(
        local, mesh=mesh, in_specs=placed, out_specs=P(None, "col", "row", None), check_vma=False
    )
```

```python
import jax
import jax.numpy as jnp
from jax import lax
from jax.experimental import pallas as pl
from jax.experimental.pallas import tpu as pltpu
from jax.sharding import PartitionSpec as P

MESH = pl.DeviceIdType.MESH
BS = 64
NNU = 384
NBNU = 128
NMB = 16
CAPM = 8
PAIRS = 64
CHUNKS = 8
EARLY = 3
AHEAD = 3
LAG = 3
HALF = 2048
F32 = jnp.float32
BF16 = jnp.bfloat16


def slot_table(mu_row, nu_row):
    sub = lax.broadcasted_iota(jnp.int32, (PAIRS, PAIRS), 0)
    lane = lax.broadcasted_iota(jnp.int32, (PAIRS, PAIRS), 1)
    mu_b = jnp.broadcast_to(mu_row, (PAIRS, PAIRS))
    nu_b = jnp.broadcast_to(nu_row, (PAIRS, PAIRS))
    mu_col = jnp.sum(jnp.where(sub == lane, mu_b, 0), axis=1, keepdims=True)
    nu_col = jnp.sum(jnp.where(sub == lane, nu_b, 0), axis=1, keepdims=True)
    rank = jnp.sum(jnp.where((mu_b == mu_col) & (lane < sub), 1, 0), axis=1, keepdims=True)
    slot = lax.broadcasted_iota(jnp.int32, (PAIRS, NMB * CAPM), 1)
    pair = lax.broadcasted_iota(jnp.int32, (PAIRS, NMB * CAPM), 0)
    hit = (mu_col * CAPM + rank) == slot
    source = jnp.sum(jnp.where(hit, pair, 0), axis=0, keepdims=True)
    target = jnp.sum(jnp.where(hit, nu_col - NBNU, 0), axis=0, keepdims=True) + NBNU
    row = lax.broadcasted_iota(jnp.int32, (8, NMB * CAPM), 0)
    return jnp.where(row == 0, source, target)


def kernel(t_ref, mu_hbm, nu_hbm, occ_ref, out_ref,
           mu_ref, nu_ref, own, arr_c, arr_d, occ, xown, xt, sums, csums, cbuf, crecv, tbuf, sbuf, rbuf, keep, gown, grecv, hbuf, gbuf, tab_v, tab_r, tab_s,
           occ_sem, own_sem, sc, rc, sd, rd, st, rt, tab_sem, sp, rp, s2, r2, sg, rg, s3, r3, sl, rl, small_sem, out_sem):
    row, col = lax.axis_index("row"), lax.axis_index("col")
    x, y, z, core = col // 4, col % 4, row // 2, row % 2

    def at_x(d):
        return (row, lax.rem(x + d, 4) * 4 + y)

    def at_y(d):
        return (row, x * 4 + lax.rem(y + d, 4))

    def ring(h, d):
        return at_x(d) if h == 0 else at_y(d)

    def place(h):
        return x if h == 0 else y

    def piece(h, d, first, count):
        if h == 0:
            return t_ref.at[lax.rem(x + d, 4), pl.ds(first, count), :, pl.ds(0, HALF)]
        return t_ref.at[pl.ds(first, count), lax.rem(y + d, 4), :, pl.ds(HALF, HALF)]

    barrier = pltpu.get_barrier_semaphore()
    for d in range(1, 4):
        pl.semaphore_signal(barrier, inc=1, device_id=at_x(d), device_id_type=MESH)
        pl.semaphore_signal(barrier, inc=1, device_id=at_y(d), device_id_type=MESH)
    for d in range(1, 8):
        pl.semaphore_signal(barrier, inc=1, device_id=(lax.rem(row + d, 8), col), device_id_type=MESH)

    small = []
    for k, (src, dst) in enumerate(((mu_hbm, mu_ref), (nu_hbm, nu_ref))):
        copy = pltpu.make_async_copy(src, dst, small_sem.at[k])
        copy.start()
        small.append(copy)
    locals_ = []
    for h in range(2):
        for k, (d, first, count, at) in enumerate(((0, 0, 4, 0), (1, 0, 2, 4), (3, 2, 2, 6))):
            copy = pltpu.make_async_copy(piece(h, d, first, count), own.at[h, pl.ds(at, count)], own_sem.at[h, k])
            copy.start()
            locals_.append(copy)
    occ_copy = pltpu.make_async_copy(occ_ref, occ.at[pl.ds(0, NBNU)], occ_sem)
    occ_copy.start()

    pl.semaphore_wait(barrier, 13)

    cs, ds, tabs = {}, {}, {}
    for w in range(2):
        for h in range(2):
            cs[h, w] = pltpu.make_async_remote_copy(
                src_ref=piece(h, 2, 2 * w, 2), dst_ref=arr_c.at[h * 2 + w], send_sem=sc.at[h, w], recv_sem=rc.at[h, w],
                device_id=ring(h, 1 + 2 * w), device_id_type=MESH)
            ds[h, w] = pltpu.make_async_remote_copy(
                src_ref=piece(h, 1 + 2 * w, 2 - 2 * w, 2), dst_ref=arr_d.at[h * 2 + w], send_sem=sd.at[h, w], recv_sem=rd.at[h, w],
                device_id=ring(h, 1 + 2 * w), device_id_type=MESH)
            cs[h, w].start()

    for copy in small:
        copy.wait()
    tab_v[...] = slot_table(mu_ref[...], nu_ref[...])
    tab_r[4] = tab_v[...]
    for w in range(2):
        for h in range(2):
            copy = pltpu.make_async_remote_copy(
                src_ref=tab_v, dst_ref=tab_r.at[h * 2 + w], send_sem=st.at[h, w], recv_sem=rt.at[h, w],
                device_id=ring(h, 1 + 2 * w), device_id_type=MESH)
            copy.start()
            tabs[h, w] = copy
    occ[NBNU] = jnp.zeros((BS, NNU), BF16)

    def relayout(src, dst, aux_count):
        def body(i, _):
            a, s0 = i // 4, pl.multiple_of(lax.rem(i, 4) * 16, 16)
            dst[pl.ds(s0, 16), pl.ds(pl.multiple_of(a * 16, 16), 16), :] = src[a, pl.ds(s0, 16), :].reshape(16, 16, 128)
            return 0
        lax.fori_loop(0, aux_count * 4, body, 0, unroll=2)

    for copy in locals_:
        copy.wait()
    for h in range(2):
        relayout(own.at[h], xown.at[h], 8)
    for copy in ds.values():
        copy.start()
    for copy in tabs.values():
        copy.wait_recv()
    tab_copy = pltpu.make_async_copy(tab_r, tab_s, tab_sem)
    tab_copy.start()
    tab_copy.wait()
    occ_copy.wait()

    def product(blocks, k, m):
        even, odd, dens = [], [], []
        for q in range(0, CAPM, 2):
            t0 = blocks[tab_s[k, 0, m * CAPM + q]]
            t1 = blocks[tab_s[k, 0, m * CAPM + q + 1]]
            even.append(jnp.concatenate([t0[:, :64], t1[:, :64]], axis=1))
            odd.append(jnp.concatenate([t0[:, 64:], t1[:, 64:]], axis=1))
            dens.append(occ[tab_s[k, 1, m * CAPM + q]])
            dens.append(occ[tab_s[k, 1, m * CAPM + q + 1]])
        left = jnp.concatenate([jnp.concatenate(even, axis=1), jnp.concatenate(odd, axis=1)], axis=0)
        right = jnp.concatenate(dens, axis=0)
        return jnp.dot(left, right, preferred_element_type=F32)

    def own_body(m, _):
        for h in range(2):
            value = product(xown.at[h], 4, m).reshape(2, 8, 16, NNU)
            sums[h, m] = value[:, 0:4]
            csums[h * 2, m] = value[:, 4:6]
            csums[h * 2 + 1, m] = value[:, 6:8]
        return 0
    lax.fori_loop(0, 4, own_body, 0, unroll=2)
    lax.fori_loop(4, NMB, own_body, 0, unroll=2)

    for u in range(4):
        cs[u // 2, u % 2].wait_recv()
        relayout(arr_c.at[u], xt.at[u], 2)

    def chunk_row(t):
        return lax.rem(z + t // 2 + 1, 4) * 2 + lax.rem(t + 1 + core, 2)

    def pair_copy(u, t):
        return pltpu.make_async_remote_copy(
            src_ref=cbuf.at[u, t], dst_ref=crecv.at[u, t], send_sem=sp.at[u, t], recv_sem=rp.at[u, t],
            device_id=ring(u // 2, 1 + 2 * (u % 2)), device_id_type=MESH)

    def start_pair(t):
        for u in range(4):
            pair_copy(u, t).start()

    def c_body(t, _):
        mu0 = chunk_row(t) * 2
        for u in range(4):
            for i in range(2):
                value = product(xt.at[u], u, mu0 + i).reshape(2, 2, 16, NNU)
                cbuf[u, t, i] = (value + csums[u, mu0 + i]).astype(BF16)

        @pl.when(t < EARLY)
        def _():
            start_pair(t)
        return 0
    lax.fori_loop(0, CHUNKS, c_body, 0)

    for copy in ds.values():
        copy.wait_send()
    for t in range(EARLY, AHEAD):
        start_pair(t)
    for copy in [*cs.values(), *tabs.values()]:
        copy.wait_send()
    for u in range(4):
        ds[u // 2, u % 2].wait_recv()
        relayout(arr_d.at[u], xt.at[u], 2)

    def direct(m):
        for u in range(4):
            h, w = u // 2, u % 2
            value = product(xt.at[u], u, m).reshape(2, 2, 16, NNU)
            sums[h, m, :, pl.ds(2 - 2 * w, 2)] += value

    def outer(h, w, t):
        return pltpu.make_async_remote_copy(
            src_ref=sbuf.at[h, w, t], dst_ref=rbuf.at[h, w, t], send_sem=s2.at[h, w, t], recv_sem=r2.at[h, w, t],
            device_id=ring(1 - h, 1 + 2 * w), device_id_type=MESH)

    def inner(h, w, t):
        return pltpu.make_async_remote_copy(
            src_ref=gown.at[h, w, t], dst_ref=grecv.at[h, w, t], send_sem=sg.at[h, w, t], recv_sem=rg.at[h, w, t],
            device_id=ring(1 - h, 1 + 2 * w), device_id_type=MESH)

    LAST = CHUNKS - 1

    def straight(h, w, k):
        return pltpu.make_async_remote_copy(
            src_ref=sbuf.at[h, w, LAST, k], dst_ref=rbuf.at[h, w, LAST, k], send_sem=sl.at[h, w, k], recv_sem=rl.at[h, w, k],
            device_id=ring(1 - h, 2 if k == 0 else 1 + 2 * w), device_id_type=MESH)

    def third(t):
        return pltpu.make_async_remote_copy(
            src_ref=hbuf.at[t], dst_ref=gbuf.at[row], send_sem=s3.at[t], recv_sem=r3.at[t],
            device_id=(chunk_row(t), col), device_id_type=MESH)

    def forward(t):
        for h in range(2):
            for w in range(2):
                outer(h, w, t).wait()
                gown[h, w, t] = (keep[h, w, t] + rbuf[h, w, t, 0].astype(F32)).astype(BF16)
                inner(h, w, t).start()

    def finish(t, last=False):
        for h in range(2):
            for w in range(2):
                inner(h, w, t).wait()
                if last:
                    for k in range(2):
                        straight(h, w, k).wait()
            for i in range(2):
                total = tbuf[h, t, i] + grecv[h, i, t].astype(F32) + rbuf[h, 1 - i, t, 1].astype(F32)
                if last:
                    total = total + rbuf[h, i, t, 0].astype(F32)
                hbuf[t, pl.ds((i * 2 + h) * 32, 32), :] = total.reshape(32, NNU).astype(BF16)

    def chunk(t, last):
        mu0 = chunk_row(t) * 2
        for i in range(2):
            direct(mu0 + i)
        for h in range(2):
            for w in range(2):
                pair_copy(h * 2 + w, t).wait()

            def total(d, i, h=h):
                a = lax.rem(place(1 - h) + d, 4)
                return sums[h, mu0 + i, :, a] + crecv[h * 2 + a // 2, t, i, :, lax.rem(a, 2)].astype(F32)
            for w in range(2):
                sbuf[h, w, t, 0] = total(2, w).astype(BF16)
                sbuf[h, w, t, 1] = total(1 + 2 * w, 1 - w).astype(BF16)
                if last:
                    for k in range(2):
                        straight(h, w, k).start()
                else:
                    outer(h, w, t).start()
            for w in range(2):
                if last:
                    gown[h, w, t] = total(1 + 2 * w, w).astype(BF16)
                    inner(h, w, t).start()
                else:
                    keep[h, w, t] = total(1 + 2 * w, w)
            for i in range(2):
                tbuf[h, t, i] = total(0, i)

    def chunk_body(t, _):
        chunk(t, False)

        @pl.when(t < CHUNKS - AHEAD)
        def _():
            start_pair(t + AHEAD)

        @pl.when(t >= 1)
        def _():
            forward(t - 1)

        @pl.when(t >= LAG)
        def _():
            finish(t - LAG)
            third(t - LAG).start()
        return 0
    lax.fori_loop(0, LAST, chunk_body, 0)
    chunk(LAST, True)
    forward(LAST - 1)
    for t in range(LAST - LAG, LAST):
        finish(t)
        third(t).start()

    def out_copy(src, g):
        return pltpu.make_async_copy(src, out_ref.at[g], out_sem.at[g])

    def last_body(t, _):
        g = lax.rem(z + 3 - t // 2, 4) * 2 + lax.rem(t + 1 + core, 2)
        third(t).wait_send()
        pltpu.make_async_remote_copy(
            src_ref=hbuf.at[t], dst_ref=gbuf.at[g], send_sem=s3.at[t], recv_sem=r3.at[t],
            device_id=(row, col), device_id_type=MESH).wait_recv()
        out_copy(gbuf.at[g], g).start()
        return 0
    lax.fori_loop(0, 6, last_body, 0)
    last_body(6, 0)
    finish(LAST, True)
    out_copy(hbuf.at[LAST], row).start()
    for g in range(8):
        out_copy(gbuf.at[g], g).wait()


def virt_kernel(virt_ref, half_ref, o_ref):
    c = lax.broadcasted_iota(jnp.int32, (128, 128), 1)
    r = lax.broadcasted_iota(jnp.int32, (128, 128), 0)
    from_col = (c // 64) * 64 + ((c // 32) % 2) * 32 + (c % 16) * 2 + (c // 16) % 2
    perm = jnp.where(r == from_col, 1.0, 0.0).astype(BF16)
    virt = jnp.dot(virt_ref[...], perm, preferred_element_type=F32).astype(BF16)
    for g in range(4):
        o_ref[g] = jnp.dot(virt, half_ref[g], preferred_element_type=F32).astype(BF16)


def local(tensor, pair_mu, pair_nu, occ_density, virt_density):
    dma = pltpu.SemaphoreType.DMA
    halves = pl.pallas_call(
        kernel,
        out_shape=jax.ShapeDtypeStruct((8, 128, NNU), BF16),
        in_specs=[
            pl.BlockSpec(memory_space=pl.ANY),
        ] * 4,
        out_specs=pl.BlockSpec(memory_space=pl.ANY),
        scratch_shapes=[
            pltpu.VMEM((1, PAIRS), jnp.int32),
            pltpu.VMEM((1, PAIRS), jnp.int32),
            pltpu.VMEM((2, 8, PAIRS, HALF), BF16),
            pltpu.VMEM((4, 2, PAIRS, HALF), BF16),
            pltpu.VMEM((4, 2, PAIRS, HALF), BF16),
            pltpu.VMEM((NBNU + 1, BS, NNU), BF16),
            pltpu.VMEM((2, PAIRS, 128, 128), BF16),
            pltpu.VMEM((4, PAIRS, 32, 128), BF16),
            pltpu.VMEM((2, NMB, 2, 4, 16, NNU), F32),
            pltpu.VMEM((4, NMB, 2, 2, 16, NNU), F32),
            pltpu.VMEM((4, CHUNKS, 2, 2, 2, 16, NNU), BF16),
            pltpu.VMEM((4, CHUNKS, 2, 2, 2, 16, NNU), BF16),
            pltpu.VMEM((2, CHUNKS, 2, 2, 16, NNU), F32),
            pltpu.VMEM((2, 2, CHUNKS, 2, 2, 16, NNU), BF16),
            pltpu.VMEM((2, 2, CHUNKS, 2, 2, 16, NNU), BF16),
            pltpu.VMEM((2, 2, CHUNKS, 2, 16, NNU), F32),
            pltpu.VMEM((2, 2, CHUNKS, 2, 16, NNU), BF16),
            pltpu.VMEM((2, 2, CHUNKS, 2, 16, NNU), BF16),
            pltpu.VMEM((8, 128, NNU), BF16),
            pltpu.VMEM((8, 128, NNU), BF16),
            pltpu.VMEM((8, 128), jnp.int32),
            pltpu.VMEM((5, 8, 128), jnp.int32),
            pltpu.SMEM((5, 8, 128), jnp.int32),
            dma, dma((2, 3)), dma((2, 2)), dma((2, 2)), dma((2, 2)), dma((2, 2)), dma((2, 2)), dma((2, 2)), dma,
            dma((4, CHUNKS)), dma((4, CHUNKS)), dma((2, 2, CHUNKS)), dma((2, 2, CHUNKS)),
            dma((2, 2, CHUNKS)), dma((2, 2, CHUNKS)), dma((7,)), dma((7,)), dma((2, 2, 2)), dma((2, 2, 2)),
            dma((2,)), dma((8,)),
        ],
        compiler_params=pltpu.CompilerParams(
            collective_id=0, has_side_effects=True, vmem_limit_bytes=60 << 20),
        name="density_transform",
    )(
        tensor.reshape(4, 4, PAIRS, BS * BS),
        pair_mu.reshape(1, PAIRS),
        pair_nu.reshape(1, PAIRS),
        occ_density.reshape(NBNU, BS, NNU),
    )
    out = pl.pallas_call(
        virt_kernel,
        out_shape=jax.ShapeDtypeStruct((8, 128, NNU), BF16),
        grid=(2,),
        in_specs=[pl.BlockSpec((128, 128), lambda g: (0, 0)), pl.BlockSpec((4, 128, NNU), lambda g: (g, 0, 0))],
        out_specs=pl.BlockSpec((4, 128, NNU), lambda g: (g, 0, 0)),
        name="virt_product",
    )(virt_density, halves)
    return out.reshape(8, 1, 128, NNU)


def solution(mesh):
    placed = (P("row", "col", None), P("col"), P("col"), P(), P("row", None))
    return jax.shard_map(
        local, mesh=mesh, in_specs=placed, out_specs=P(None, "col", "row", None), check_vma=False
    )
```
